128 devices in a mesh: heads: 4 (over y), ctx: 32 (over z, x, core).
Axes of the slice: x: 4, y: 4, z: 4, core: 2. Of those that a mesh axis runs over, the one named last changes fastest.
Arguments:
- queries: bfloat16 [8192, 8192], P(('ctx', 'heads')), may hold values from -120 to 120
- keys: bfloat16 [8192, 1024], P(('ctx', 'heads')), may hold values from -6 to 6
- values: bfloat16 [8192, 1024], P(('ctx', 'heads')), may hold values from -3 to 3
- grad_out: bfloat16 [8192, 8192], P(('ctx', 'heads')), may hold values from -1.5 to 1.5
- doc_lengths: int32 [16], replicated, may hold values from 1 to 1024, 8192 in all
- share_prefix: int32 [16], replicated, may hold values 0 or 1
Outputs:
- attn_out: bfloat16 [8192, 8192], P(('ctx', 'heads'))
- grad_queries: bfloat16 [8192, 8192], P(('ctx', 'heads'))
- grad_keys: bfloat16 [8192, 1024], P(('ctx', 'heads'))
- grad_values: bfloat16 [8192, 1024], P(('ctx', 'heads'))
The draws below stay inside these ranges and needn't reach their ends.
Inputs may be any that keep to these rules, and one draw needn't show every extreme that they name: `doc_lengths`: they sum to 8192.
All inputs are finite; a program needn't handle non-finite values.
Results may differ from the reference program's by a relative error of at most 0.035.
Values may be sent and summed in bfloat16 or wider, within the bound.
A program may use at most 128 MiB of HBM per device.

```python
import math
import jax
import jax.numpy as jnp
import numpy as np
from jax import lax

QH = 64
KVH = 8
HD = 128
TOKENS = 8192
DOCS = 16
DOC_MOST = 1024


def draw_keys(key, part):
    key = jax.random.fold_in(key, 11)
    drawn = jnp.clip(jax.random.normal(key, (TOKENS, KVH, HD), jnp.float32), -6.0, 6.0)
    return drawn.reshape(TOKENS, KVH * HD).astype(jnp.bfloat16)


def draw_queries(key, part):
    key = jax.random.fold_in(key, 12)
    per = QH // KVH
    drawn = jnp.clip(jax.random.normal(key, (TOKENS, KVH, per, HD), jnp.float32), -6.0, 6.0)
    return drawn.reshape(TOKENS, QH * HD).astype(jnp.bfloat16)


def with_ends(entries, own_key, low, top_value):
    extent = entries.shape
    index_at = [jax.random.randint(jax.random.fold_in(own_key, axis), (), 0, extent[axis]) for axis in range(len(extent))]
    entries = entries.at[tuple(index_at)].set(low)
    longest = extent.index(max(extent))
    index_at[longest] = (index_at[longest] + 1) % extent[longest]
    return entries.at[tuple(index_at)].set(top_value)


def shard_levels(key, extent, pieces, least, largest):
    def one(axis_at, blocks):
        draws = jax.random.uniform(jax.random.fold_in(jax.random.fold_in(key, 6), axis_at), (blocks,), jnp.float32, least / len(pieces), largest / len(pieces))
        return jnp.repeat(jnp.exp(draws), extent[axis_at] // blocks).reshape((-1,) + (1,) * (len(extent) - axis_at - 1))

    gain = one(*pieces[0])
    for cut in pieces[1:]:
        gain = gain * one(*cut)
    return gain


def split_up(count, total, most, lean):
    loads = [(1 << 20) // math.isqrt(standing ** lean) + 1 for standing in range(2, count + 1)]
    surplus, holding = total - most - (count - 1), [1] * (count - 1)
    while surplus > 0:
        free = [i for i in range(count - 1) if holding[i] < most]
        mass, budget = sum([loads[i] for i in free]), surplus
        for i in free:
            more = min(most - holding[i], max(1, budget * loads[i] // mass), surplus)
            holding[i] = holding[i] + more
            surplus = surplus - more
    return np.array([most] + holding)


def uneven(own_key, number_of, total, reach, lean):
    if number_of == 2:
        one = jax.random.randint(own_key, (), max(1, total - reach), min(reach, total - 1) + 1)
        return jnp.stack([one, total - one])
    tallies = jnp.asarray(split_up(number_of, total, reach, lean), jnp.int32)
    couples = (number_of - 1) // 2
    donor, sink = tallies[1:1 + 2 * couples:2], tallies[2:2 + 2 * couples:2]
    room = jnp.minimum(donor - 1, reach - sink)
    moved = jax.random.randint(jax.random.fold_in(own_key, 1), (couples,), 0, 1 << 20) % (room + 1)
    tallies = tallies.at[1:1 + 2 * couples:2].set(donor - moved).at[2:2 + 2 * couples:2].set(sink + moved)
    return tallies[jax.random.permutation(jax.random.fold_in(own_key, 2), number_of)]


def noise(stream_key, dims, deviation, bound, split=(), kind=jnp.bfloat16):
    values = deviation * jax.random.normal(stream_key, dims, jnp.float32)
    if split:
        values = values * shard_levels(stream_key, dims, split, -0.22, 0.18)
    return jnp.clip(values, -bound, bound).astype(kind)


def setup_inputs(seed: int = 0) -> dict:
    key_list = jax.random.split(jax.random.key(seed), 7)
    return {
        "queries": draw_queries(jax.random.fold_in(key_list[6], 71), 0),
        "keys": draw_keys(jax.random.fold_in(key_list[6], 71), 0),
        "values": noise(key_list[2], (TOKENS, KVH * HD), 0.5, 3.0, ((0, 128),)),
        "grad_out": noise(key_list[3], (TOKENS, QH * HD), 0.25, 1.5, ((0, 128),)),
        "doc_lengths": uneven(key_list[4], DOCS, TOKENS, DOC_MOST, 2).astype(jnp.int32),
        "share_prefix": with_ends((jax.random.randint(key_list[5], (DOCS,), 0, 2) < 1).astype(jnp.int32), jax.random.fold_in(key_list[5], 1), 0, 1),
    }


def one_head(qh, kh, vh, doh, allowed, scale):
    s = jnp.dot(qh, kh.T, preferred_element_type=jnp.float32) * scale
    s = jnp.where(allowed, s, -1e30)
    top = jnp.max(s, axis=1)
    lse = top + jnp.log(jnp.sum(jnp.where(allowed, jnp.exp(s - top[:, None]), 0.0), axis=1))
    prob = jnp.where(allowed, jnp.exp(s - lse[:, None]), 0.0)
    prob_b = prob.astype(jnp.bfloat16)
    out = jnp.dot(prob_b, vh, preferred_element_type=jnp.float32).astype(jnp.bfloat16)
    delta = jnp.sum(doh.astype(jnp.float32) * out.astype(jnp.float32), axis=1)
    dprob = jnp.dot(doh, vh.T, preferred_element_type=jnp.float32)
    dscore = (prob * (dprob - delta[:, None])).astype(jnp.bfloat16)
    dq = jnp.dot(dscore, kh, preferred_element_type=jnp.float32) * scale
    dk = jnp.dot(dscore.T, qh, preferred_element_type=jnp.float32) * scale
    dv = jnp.dot(prob_b.T, doh, preferred_element_type=jnp.float32)
    return out, dq, dk, dv


def reference(queries, keys, values, grad_out, doc_lengths, share_prefix):
    per = QH // KVH
    scale = HD ** -0.5
    pos = jnp.arange(TOKENS, dtype=jnp.int32)
    ends = jnp.cumsum(doc_lengths).astype(jnp.int32)
    doc = jnp.sum((ends[None, :] <= pos[:, None]).astype(jnp.int32), axis=1)
    share = jnp.sum(jnp.where(doc[:, None] == jnp.arange(DOCS, dtype=jnp.int32)[None, :], share_prefix[None, :], 0), axis=1)
    allowed = (pos[None, :] <= pos[:, None]) & ((doc[None, :] == doc[:, None]) | ((doc[None, :] == 0) & (share[:, None] == 1)))
    q_grp = queries.reshape(TOKENS, KVH, per, HD).transpose(1, 2, 0, 3)
    do_grp = grad_out.reshape(TOKENS, KVH, per, HD).transpose(1, 2, 0, 3)
    k_grp = keys.reshape(TOKENS, KVH, HD).transpose(1, 0, 2)
    v_grp = values.reshape(TOKENS, KVH, HD).transpose(1, 0, 2)

    def group(items):
        q_all, kh, vh, do_all = items

        def head(pair):
            return one_head(pair[0], kh, vh, pair[1], allowed, scale)

        out, dq, dk, dv = lax.map(head, (q_all, do_all))
        return out, dq.astype(jnp.bfloat16), jnp.sum(dk, axis=0).astype(jnp.bfloat16), jnp.sum(dv, axis=0).astype(jnp.bfloat16)

    out, dq, dk, dv = lax.map(group, (q_grp, k_grp, v_grp, do_grp))
    attn_out = out.transpose(2, 0, 1, 3).reshape(TOKENS, QH * HD)
    grad_queries = dq.transpose(2, 0, 1, 3).reshape(TOKENS, QH * HD)
    grad_keys = dk.transpose(1, 0, 2).reshape(TOKENS, KVH * HD)
    grad_values = dv.transpose(1, 0, 2).reshape(TOKENS, KVH * HD)
    return (attn_out, grad_queries, grad_keys, grad_values)
```

```python
import functools

import jax
import jax.numpy as jnp
from jax import lax
from jax.experimental import pallas as pl
from jax.experimental.pallas import tpu as pltpu
from jax.sharding import PartitionSpec as P

QH = 64
KVH = 8
HD = 128
PER = QH // KVH
DOCS = 16
MESH = pl.DeviceIdType.MESH
BF = jnp.bfloat16
F32 = jnp.float32

UNIT = 256
BLK = 64
BACK = 4
PRE = 1024
KEYS = PRE + (BACK + 1) * UNIT
GROUPS = 2
QCOL = GROUPS * PER * HD
KCOL = GROUPS * HD

ROWS = 128
KC = 256
NCH = KEYS // KC
LANES = PER * ROWS
SCALE = HD ** (-0.5)
LOG2E = 1.4426950408889634


def attention_kernel(
    lens, share, q_ref, do_ref, kv_ref, out_ref, dq_ref, g_ref,
    s_scr, p_scr, q_scr, dot_scr, kt_scr, vt_scr, gk_scr, gv_scr, acc_scr, m_scr, l_scr,
):
    ctx = lax.axis_index("ctx")
    first = ctx * UNIT
    base = first - BACK * UNIT - PRE

    for i in range(NCH):
        kt_scr[i] = kv_ref[0, i * KC:(i + 1) * KC, :].astype(F32).T.astype(BF)
        vt_scr[i] = kv_ref[1, i * KC:(i + 1) * KC, :].astype(F32).T.astype(BF)
    gk_scr[...] = jnp.zeros_like(gk_scr)
    gv_scr[...] = jnp.zeros_like(gv_scr)

    len0 = lens[0]

    def row_block(r, carry):
        p0 = first + r * ROWS
        row_at = pl.multiple_of(r * ROWS, ROWS)
        end = jnp.int32(0)
        own = jnp.int32(0)
        last = jnp.int32(0)
        reads = jnp.int32(0)
        pos = p0 + lax.broadcasted_iota(jnp.int32, (1, LANES), 1) % ROWS
        start_i = jnp.zeros((1, LANES), jnp.int32)
        share_i = jnp.zeros((1, LANES), jnp.int32)
        for d in range(DOCS):
            begin = end
            end = begin + lens[d]
            own = jnp.where(p0 >= begin, begin, own)
            last = jnp.where(p0 + ROWS - 1 >= begin, begin, last)
            inside = pos >= begin
            start_i = jnp.where(inside, begin, start_i)
            if d > 0:
                share_i = jnp.where(inside, share[d], share_i)
                touch = (begin < p0 + ROWS) & (end > p0) & (share[d] == 1)
                reads = jnp.where(touch, jnp.int32(1), reads)
        plim_i = jnp.where(share_i == 1, len0, 0)
        n_pre = jnp.where(reads == 1, (len0 + KC - 1) // KC, 0)
        w_lo = (own - base) // KC
        w_hi = (p0 + ROWS - 1 - base) // KC
        total = n_pre + w_hi - w_lo + 1
        wstart_i = start_i - base
        wend_i = pos - base
        full_lo = last - base
        full_hi = p0 - base

        for h in range(PER):
            q_scr[h * ROWS:(h + 1) * ROWS, :] = q_ref[pl.ds(row_at, ROWS), h * HD:(h + 1) * HD]
        m_scr[...] = jnp.full_like(m_scr, -1e30)
        l_scr[...] = jnp.zeros_like(l_scr)

        def chunk_of(t):
            return jnp.where(t < n_pre, t, t - n_pre + w_lo)

        def score_step(t, carry):
            i = chunk_of(t)
            at = pl.multiple_of(i * KC, KC)
            in_pre = t < n_pre
            s = lax.dot_general(
                kv_ref[0, pl.ds(at, KC), :], q_scr[...], (((1,), (1,)), ((), ())),
                preferred_element_type=F32,
            )
            whole = (i * KC >= full_lo) & (i * KC + KC - 1 <= full_hi) & jnp.logical_not(in_pre)

            @pl.when(whole)
            def _():
                s_scr[pl.ds(at, KC), :] = s
                m_scr[...] = jnp.maximum(m_scr[...], jnp.max(s.reshape(KC // 8, 8, LANES), axis=0))

            @pl.when(jnp.logical_not(whole))
            def _():
                j = i * KC + lax.broadcasted_iota(jnp.int32, (KC, LANES), 0)
                lo = jnp.where(in_pre, 0, wstart_i)
                hi = jnp.where(in_pre, plim_i - 1, wend_i)
                sm = jnp.where((j >= lo) & (j <= hi), s, -1e30)
                s_scr[pl.ds(at, KC), :] = sm
                m_scr[...] = jnp.maximum(m_scr[...], jnp.max(sm.reshape(KC // 8, 8, LANES), axis=0))

            return carry

        lax.fori_loop(0, total, score_step, 0)
        mc = jnp.max(m_scr[...], axis=0, keepdims=True) * (SCALE * LOG2E)
        acc_scr[...] = jnp.zeros_like(acc_scr)

        def value_step(t, carry):
            i = chunk_of(t)
            at = pl.multiple_of(i * KC, KC)
            p = jnp.exp2(s_scr[pl.ds(at, KC), :] * (SCALE * LOG2E) - mc)
            l_scr[...] += jnp.sum(p.reshape(KC // 8, 8, LANES), axis=0)
            pb = p.astype(BF)
            p_scr[pl.ds(at, KC), :] = pb
            acc_scr[...] += jnp.dot(vt_scr[i], pb, preferred_element_type=F32)
            return carry

        lax.fori_loop(0, total, value_step, 0)
        inv = 1.0 / jnp.sum(l_scr[...], axis=0, keepdims=True)
        out_t = acc_scr[...] * inv
        out = out_t.T.astype(BF)
        do_parts = []
        for h in range(PER):
            out_ref[pl.ds(row_at, ROWS), h * HD:(h + 1) * HD] = out[h * ROWS:(h + 1) * ROWS, :]
            do_parts.append(
                do_ref[pl.ds(row_at, ROWS), h * HD:(h + 1) * HD].astype(F32).T
            )
        do_t = (jnp.concatenate(do_parts, axis=1) * inv).astype(BF)
        dot_scr[...] = do_t
        delta = jnp.sum(do_t.astype(F32) * out_t.astype(BF).astype(F32), axis=0, keepdims=True)
        acc_scr[...] = jnp.zeros_like(acc_scr)

        def back_step(t, carry):
            i = chunk_of(t)
            at = pl.multiple_of(i * KC, KC)
            dp = jnp.dot(kv_ref[1, pl.ds(at, KC), :], dot_scr[...], preferred_element_type=F32)
            pb = p_scr[pl.ds(at, KC), :]
            ds = (pb.astype(F32) * (dp - delta)).astype(BF)
            gv_scr[pl.ds(at, KC), :] += lax.dot_general(
                pb, dot_scr[...], (((1,), (1,)), ((), ())), preferred_element_type=F32
            )
            gk_scr[pl.ds(at, KC), :] += jnp.dot(ds, q_scr[...], preferred_element_type=F32)
            acc_scr[...] += jnp.dot(kt_scr[i], ds, preferred_element_type=F32)
            return carry

        lax.fori_loop(0, total, back_step, 0)
        dq = (acc_scr[...] * SCALE).T.astype(BF)
        for h in range(PER):
            dq_ref[pl.ds(row_at, ROWS), h * HD:(h + 1) * HD] = dq[h * ROWS:(h + 1) * ROWS, :]
        return carry

    lax.fori_loop(0, UNIT // ROWS, row_block, 0)
    g_ref[0] = (gk_scr[...] * SCALE).astype(BF)
    g_ref[1] = gv_scr[...].astype(BF)


def attention(q, do, kv, lens, share):
    wide = pl.BlockSpec((UNIT, PER * HD), lambda g: (0, g))
    keys = pl.BlockSpec((2, KEYS, HD), lambda g: (0, 0, g))
    smem = pl.BlockSpec(memory_space=pltpu.SMEM)
    return pl.pallas_call(
        attention_kernel,
        grid=(GROUPS,),
        in_specs=[smem, smem, wide, wide, keys],
        out_specs=[wide, wide, keys],
        out_shape=[
            jax.ShapeDtypeStruct((UNIT, QCOL), BF),
            jax.ShapeDtypeStruct((UNIT, QCOL), BF),
            jax.ShapeDtypeStruct((2, KEYS, KCOL), BF),
        ],
        scratch_shapes=[
            pltpu.VMEM((KEYS, LANES), F32),
            pltpu.VMEM((KEYS, LANES), BF),
            pltpu.VMEM((LANES, HD), BF),
            pltpu.VMEM((HD, LANES), BF),
            pltpu.VMEM((NCH, HD, KC), BF),
            pltpu.VMEM((NCH, HD, KC), BF),
            pltpu.VMEM((KEYS, HD), F32),
            pltpu.VMEM((KEYS, HD), F32),
            pltpu.VMEM((HD, LANES), F32),
            pltpu.VMEM((8, LANES), F32),
            pltpu.VMEM((8, LANES), F32),
        ],
        compiler_params=pltpu.CompilerParams(vmem_limit_bytes=56 * 1024 * 1024),
        name="attention",
    )(lens, share, q, do, kv)


def place():
    ctx = lax.axis_index("ctx")
    y = lax.axis_index("heads")
    core = ctx % 2
    slab = ctx // 2
    return ctx, y, core, slab, slab // 4, slab % 4


def device(slab, core, y):
    return {"ctx": slab * 2 + core, "heads": y}


def gather_kernel(
    q_ref, do_ref, k_ref, v_ref, qg_ref, dog_ref, kv_ref,
    send, recv_q, recv_kv, recv_win, recv_core, recv_piece, recv_x, recv_z, local,
):
    ctx, y, core, slab, z, x = place()
    sibling = device(slab, 1 - core, y)
    barrier = pltpu.get_barrier_semaphore()
    for step in range(1, 4):
        pl.semaphore_signal(barrier, inc=1, device_id=device(slab, core, (y + step) % 4), device_id_type=MESH)
        pl.semaphore_signal(barrier, inc=1, device_id=device(z * 4 + (x + step) % 4, core, y), device_id_type=MESH)
        pl.semaphore_signal(barrier, inc=1, device_id=device((slab + 4 * step) % 16, core, y), device_id_type=MESH)
    for step in (1, 2, 14, 15):
        pl.semaphore_signal(barrier, inc=1, device_id=device((slab + step) % 16, core, y), device_id_type=MESH)
    pl.semaphore_signal(barrier, inc=1, device_id=sibling, device_id_type=MESH)
    source = (z == 0) & (x < 2)
    origin = z // 2

    @pl.when(source)
    def _():
        for i in range(8):
            @pl.when(8 * x + i != slab)
            def _():
                pl.semaphore_signal(barrier, inc=1, device_id=device(8 * x + i, core, y), device_id_type=MESH)

    @pl.when(slab != origin)
    def _():
        pl.semaphore_signal(barrier, inc=1, device_id=device(origin, core, y), device_id_type=MESH)

    pl.semaphore_wait(barrier, 14 + jnp.where(slab == 0, 7, jnp.where(slab == 1, 9, 1)))

    own = PRE + BACK * UNIT
    mine = pl.multiple_of(y * BLK, BLK)

    copies = []
    here = []
    for n, ref in enumerate((k_ref, v_ref)):
        for step in range(1, 4):
            to = (y + step) % 4
            col = pl.multiple_of(to * KCOL, KCOL)
            copy = pltpu.make_async_remote_copy(
                src_ref=ref.at[:, pl.ds(col, KCOL)],
                dst_ref=kv_ref.at[n, pl.ds(own + mine, BLK), :],
                send_sem=send.at[n * 3 + step - 1],
                recv_sem=recv_kv.at[n * 3 + step - 1],
                device_id=device(slab, core, to),
                device_id_type=MESH,
            )
            copy.start()
            copies.append(copy)
        col = pl.multiple_of(y * KCOL, KCOL)
        copy = pltpu.make_async_copy(
            ref.at[:, pl.ds(col, KCOL)], kv_ref.at[n, pl.ds(own + mine, BLK), :], local.at[n]
        )
        copy.start()
        here.append(copy)
    kv_copies = copies
    q_copies = []
    for n, (ref, out) in enumerate(((q_ref, qg_ref), (do_ref, dog_ref))):
        for step in range(1, 4):
            to = (y + step) % 4
            col = pl.multiple_of(to * QCOL, QCOL)
            copy = pltpu.make_async_remote_copy(
                src_ref=ref.at[:, pl.ds(col, QCOL)],
                dst_ref=out.at[pl.ds(mine, BLK), :],
                send_sem=send.at[6 + n * 3 + step - 1],
                recv_sem=recv_q.at[n * 3 + step - 1],
                device_id=device(slab, core, to),
                device_id_type=MESH,
            )
            copy.start()
            q_copies.append(copy)
        col = pl.multiple_of(y * QCOL, QCOL)
        copy = pltpu.make_async_copy(
            ref.at[:, pl.ds(col, QCOL)], out.at[pl.ds(mine, BLK), :], local.at[2 + n]
        )
        copy.start()
        here.append(copy)
    here[0].wait()
    here[1].wait()
    for copy in kv_copies:
        copy.wait_recv()

    def rows(at, count):
        return kv_ref.at[:, pl.ds(at, count), :]

    def send_rows(src, dst, count, send_sem, recv_sem, to):
        return pltpu.make_async_remote_copy(
            src_ref=rows(src, count), dst_ref=rows(dst, count), send_sem=send_sem,
            recv_sem=recv_sem, device_id=to, device_id_type=MESH,
        )

    slot = [PRE + i * UNIT for i in range(BACK + 1)]
    part = 32
    piece = (core + 2 * origin) * UNIT + (slab % 8) * part
    piece = pl.multiple_of(piece, part)

    def scatter(i):
        return send_rows(
            pl.multiple_of(own + i * part, part),
            pl.multiple_of((core + 2 * x) * UNIT + i * part, part),
            part, send.at[12 + i], recv_piece, device(8 * x + i, core, y),
        )

    own_piece = pltpu.make_async_copy(
        rows(own, part), rows(pl.multiple_of(core * UNIT, part), part), local.at[4]
    )

    @pl.when(source)
    def _():
        for i in range(8):
            @pl.when(8 * x + i != slab)
            def _():
                scatter(i).start()

    @pl.when(slab == 0)
    def _():
        own_piece.start()

    def window(ahead):
        return send_rows(
            own, slot[2] if ahead == 1 else slot[0], UNIT, send.at[20 + ahead], recv_win.at[ahead - 1],
            device((slab + ahead) % 16, core, y),
        )

    for ahead in (1, 2):
        @pl.when(slab + ahead < 16)
        def _():
            window(ahead).start()

    core_own = send_rows(own, slot[3], UNIT, send.at[23], recv_core.at[0], sibling)

    @pl.when(core == 0)
    def _():
        core_own.start()

    @pl.when(slab == 0)
    def _():
        own_piece.wait()

    @pl.when(slab != 0)
    def _():
        send_rows(piece, piece, part, send.at[12], recv_piece, sibling).wait_recv()

    x_copies = []
    for step in range(1, 4):
        copy = send_rows(
            piece, piece, part, send.at[24 + step - 1], recv_x.at[step - 1],
            device(z * 4 + (x + step) % 4, core, y),
        )
        copy.start()
        x_copies.append(copy)
    for copy in x_copies:
        copy.wait_recv()
    plane = pl.multiple_of((core + 2 * origin) * UNIT + (z % 2) * 4 * part, 4 * part)
    z_copies = []
    for step in range(1, 4):
        copy = send_rows(
            plane, plane, 4 * part, send.at[27 + step - 1], recv_z.at[step - 1],
            device((slab + 4 * step) % 16, core, y),
        )
        copy.start()
        z_copies.append(copy)
    pass_near = [
        send_rows(slot[2], slot[1], UNIT, send.at[30], recv_core.at[1], sibling),
        send_rows(slot[2], slot[3], UNIT, send.at[30], recv_core.at[0], sibling),
    ]
    pass_far = send_rows(slot[0], slot[1], UNIT, send.at[31], recv_core.at[1], sibling)

    @pl.when(slab >= 1)
    def _():
        window(1).wait_recv()

        @pl.when(core == 0)
        def _():
            pass_near[0].start()

        @pl.when(core == 1)
        def _():
            pass_near[1].start()

    @pl.when(slab >= 2)
    def _():
        window(2).wait_recv()

        @pl.when(core == 1)
        def _():
            pass_far.start()

    for copy in z_copies:
        copy.wait_recv()
    halves = []
    for i in range(2):
        at = pl.multiple_of((core + 2 * i) * UNIT, UNIT)
        copy = send_rows(at, at, UNIT, send.at[32 + i], recv_core.at[2 + i], sibling)
        copy.start()
        halves.append(copy)

    for copy in q_copies:
        copy.wait_recv()
    here[2].wait()
    here[3].wait()
    for copy in halves:
        copy.wait_recv()

    @pl.when(core == 1)
    def _():
        core_own.wait_recv()

        @pl.when(slab >= 1)
        def _():
            pass_near[0].wait_recv()

    @pl.when(core == 0)
    def _():
        @pl.when(slab >= 1)
        def _():
            pass_near[1].wait_recv()

        @pl.when(slab >= 2)
        def _():
            pass_far.wait_recv()

    for copy in kv_copies + q_copies + x_copies + z_copies + halves:
        copy.wait_send()

    @pl.when(source)
    def _():
        for i in range(8):
            @pl.when(8 * x + i != slab)
            def _():
                scatter(i).wait_send()

    for ahead in (1, 2):
        @pl.when(slab + ahead < 16)
        def _():
            window(ahead).wait_send()

    @pl.when(core == 0)
    def _():
        core_own.wait_send()

    @pl.when(slab >= 1)
    def _():
        pass_near[0].wait_send()

    @pl.when((slab >= 2) & (core == 1))
    def _():
        pass_far.wait_send()


def gather(q, do, k, v):
    any_spec = pl.BlockSpec(memory_space=pl.ANY)
    return pl.pallas_call(
        gather_kernel,
        in_specs=[any_spec] * 4,
        out_specs=[any_spec] * 3,
        out_shape=[
            jax.ShapeDtypeStruct((UNIT, QCOL), BF),
            jax.ShapeDtypeStruct((UNIT, QCOL), BF),
            jax.ShapeDtypeStruct((2, KEYS, KCOL), BF),
        ],
        scratch_shapes=[
            pltpu.SemaphoreType.DMA((34,)),
            pltpu.SemaphoreType.DMA((6,)),
            pltpu.SemaphoreType.DMA((6,)),
            pltpu.SemaphoreType.DMA((2,)),
            pltpu.SemaphoreType.DMA((4,)),
            pltpu.SemaphoreType.DMA,
            pltpu.SemaphoreType.DMA((3,)),
            pltpu.SemaphoreType.DMA((3,)),
            pltpu.SemaphoreType.DMA((5,)),
        ],
        compiler_params=pltpu.CompilerParams(collective_id=0, has_side_effects=True),
        name="gather",
    )(q, do, k, v)


def reduce_kernel(
    out_ref, dq_ref, g_ref, o_ref, odq_ref, dk_ref, dv_ref,
    own_buf, core_buf, z_send, z_buf, x_send, x_buf, last_send, last_buf, w_send, w_buf, sum_buf, k_buf,
    send, recv_q, recv_core, recv_z, recv_x, recv_last, recv_win, recv_k, local,
):
    ctx, y, core, slab, z, x = place()
    sibling = device(slab, 1 - core, y)
    barrier = pltpu.get_barrier_semaphore()
    for step in range(1, 4):
        pl.semaphore_signal(barrier, inc=1, device_id=device(slab, core, (y + step) % 4), device_id_type=MESH)
        pl.semaphore_signal(barrier, inc=1, device_id=device(z * 4 + (x + step) % 4, core, y), device_id_type=MESH)
        pl.semaphore_signal(barrier, inc=1, device_id=device((slab + 4 * step) % 16, core, y), device_id_type=MESH)
    for step in (1, 2, 14, 15):
        pl.semaphore_signal(barrier, inc=1, device_id=device((slab + step) % 16, core, y), device_id_type=MESH)
    pl.semaphore_signal(barrier, inc=1, device_id=sibling, device_id_type=MESH)
    source = (z == 0) & (x < 2)
    origin = z // 2

    @pl.when(source)
    def _():
        for i in range(8):
            @pl.when(8 * x + i != slab)
            def _():
                pl.semaphore_signal(barrier, inc=1, device_id=device(8 * x + i, core, y), device_id_type=MESH)

    @pl.when(slab != origin)
    def _():
        pl.semaphore_signal(barrier, inc=1, device_id=device(origin, core, y), device_id_type=MESH)

    pl.semaphore_wait(barrier, 14 + jnp.where(slab == 0, 7, jnp.where(slab == 1, 9, 1)))

    mine = pl.multiple_of(y * BLK, BLK)

    def g_rows(at, count):
        return g_ref.at[:, pl.ds(at, count), :]

    def remote(src, dst, send_sem, recv_sem, to):
        return pltpu.make_async_remote_copy(
            src_ref=src, dst_ref=dst, send_sem=send_sem, recv_sem=recv_sem,
            device_id=to, device_id_type=MESH,
        )

    core_copies = []
    for i in range(2):
        at = pl.multiple_of((1 - core + 2 * i) * UNIT, UNIT)
        copy = remote(g_rows(at, UNIT), core_buf.at[i], send.at[i], recv_core.at[i], sibling)
        copy.start()
        core_copies.append(copy)
    for i in range(2):
        copy = remote(
            g_rows(PRE + (1 + 2 * i) * UNIT, UNIT), core_buf.at[2 + i], send.at[2 + i], recv_core.at[2 + i], sibling
        )
        copy.start()
        core_copies.append(copy)
    loads = []
    for i in range(2):
        at = pl.multiple_of((core + 2 * i) * UNIT, UNIT)
        copy = pltpu.make_async_copy(g_rows(at, UNIT), own_buf.at[i], local.at[i])
        copy.start()
        loads.append(copy)
    for i in range(3):
        copy = pltpu.make_async_copy(g_rows(PRE + 2 * i * UNIT, UNIT), own_buf.at[2 + i], local.at[2 + i])
        copy.start()
        loads.append(copy)

    q_copies = []
    here = []
    for n, (ref, out) in enumerate(((out_ref, o_ref), (dq_ref, odq_ref))):
        for step in range(1, 4):
            to = (y + step) % 4
            col = pl.multiple_of(y * QCOL, QCOL)
            copy = remote(
                ref.at[pl.ds(pl.multiple_of(to * BLK, BLK), BLK), :],
                out.at[:, pl.ds(col, QCOL)],
                send.at[4 + n * 3 + step - 1], recv_q.at[n * 3 + step - 1], device(slab, core, to),
            )
            copy.start()
            q_copies.append(copy)
        copy = pltpu.make_async_copy(
            ref.at[pl.ds(mine, BLK), :],
            out.at[:, pl.ds(pl.multiple_of(y * QCOL, QCOL), QCOL)],
            local.at[5 + n],
        )
        copy.start()
        here.append(copy)

    part = 32
    for i in range(2):
        loads[i].wait()
        core_copies[i].wait_recv()
        z_send[i] = (own_buf[i].astype(F32) + core_buf[i].astype(F32)).astype(BF)
    z_copies = []
    for step in range(1, 4):
        to = (z + step) % 4
        at = pl.multiple_of((to % 2) * 4 * part, 4 * part)
        copy = remote(
            z_send.at[to // 2, :, pl.ds(at, 4 * part), :], z_buf.at[step - 1],
            send.at[10 + step - 1], recv_z.at[step - 1], device((slab + 4 * step) % 16, core, y),
        )
        copy.start()
        z_copies.append(copy)

    for i in range(3):
        loads[2 + i].wait()
    core_copies[2].wait_recv()
    core_copies[3].wait_recv()
    a = core_buf[2].astype(F32)
    b = core_buf[3].astype(F32)
    lower = core == 0
    far = own_buf[2].astype(F32)
    near = own_buf[3].astype(F32)
    w_send[0] = (near + jnp.where(lower, a, b)).astype(BF)
    w_send[1] = jnp.where(lower, far, far + a).astype(BF)
    sum_buf[...] = own_buf[4].astype(F32) + jnp.where(lower, b, 0.0)

    def window(back):
        return remote(
            w_send.at[back - 1], w_buf.at[back - 1], send.at[13 + back], recv_win.at[back - 1],
            device((slab + 16 - back) % 16, core, y),
        )

    for back in (1, 2):
        @pl.when(slab >= back)
        def _():
            window(back).start()

    for copy in z_copies:
        copy.wait_recv()
    at = pl.multiple_of((z % 2) * 4 * part, 4 * part)
    total = z_send[z // 2, :, pl.ds(at, 4 * part), :].astype(F32)
    for i in range(3):
        total += z_buf[i].astype(F32)
    x_send[...] = total.astype(BF)
    x_copies = []
    for step in range(1, 4):
        to = (x + step) % 4
        copy = remote(
            x_send.at[:, pl.ds(pl.multiple_of(to * part, part), part), :], x_buf.at[step - 1],
            send.at[16 + step - 1], recv_x.at[step - 1], device(z * 4 + to, core, y),
        )
        copy.start()
        x_copies.append(copy)
    for copy in x_copies:
        copy.wait_recv()
    total = x_send[:, pl.ds(pl.multiple_of(x * part, part), part), :].astype(F32)
    for i in range(3):
        total += x_buf[i].astype(F32)
    last_send[...] = total.astype(BF)

    at = pl.multiple_of((slab % 8) * part, part)
    home = remote(last_send, last_buf.at[:, pl.ds(at, part), :], send.at[19], recv_last.at[slab % 8], device(origin, core, y))

    def arrival(i):
        return remote(last_send, last_buf.at[:, pl.ds(i * part, part), :], send.at[19], recv_last.at[i], sibling)

    @pl.when(slab != origin)
    def _():
        home.start()

    for back in (1, 2):
        @pl.when(slab + back < 16)
        def _():
            window(back).wait_recv()
            sum_buf[...] += w_buf[back - 1].astype(F32)

    @pl.when(source)
    def _():
        for i in range(8):
            @pl.when(8 * x + i != slab)
            def _():
                arrival(i).wait_recv()

        @pl.when(slab == 0)
        def _():
            last_buf[:, 0:part, :] = last_send[...]

        sum_buf[...] += last_buf[...].astype(F32)

    k_buf[...] = sum_buf[...].astype(BF)
    k_copies = []
    col = pl.multiple_of(y * KCOL, KCOL)
    for n, out in enumerate((dk_ref, dv_ref)):
        for step in range(1, 4):
            to = (y + step) % 4
            copy = remote(
                k_buf.at[n, pl.ds(pl.multiple_of(to * BLK, BLK), BLK), :], out.at[:, pl.ds(col, KCOL)],
                send.at[20 + n * 3 + step - 1], recv_k.at[n * 3 + step - 1], device(slab, core, to),
            )
            copy.start()
            k_copies.append(copy)
        copy = pltpu.make_async_copy(k_buf.at[n, pl.ds(mine, BLK), :], out.at[:, pl.ds(col, KCOL)], local.at[7 + n])
        copy.start()
        here.append(copy)

    for copy in here:
        copy.wait()
    for copy in q_copies + k_copies:
        copy.wait_recv()
    for copy in core_copies + q_copies + z_copies + x_copies + k_copies:
        copy.wait_send()

    @pl.when(slab != origin)
    def _():
        home.wait_send()

    for back in (1, 2):
        @pl.when(slab >= back)
        def _():
            window(back).wait_send()


def reduce(out, dq, g):
    any_spec = pl.BlockSpec(memory_space=pl.ANY)
    unit = (2, UNIT, KCOL)
    return pl.pallas_call(
        reduce_kernel,
        in_specs=[any_spec] * 3,
        out_specs=[any_spec] * 4,
        out_shape=[
            jax.ShapeDtypeStruct((BLK, QH * HD), BF),
            jax.ShapeDtypeStruct((BLK, QH * HD), BF),
            jax.ShapeDtypeStruct((BLK, KVH * HD), BF),
            jax.ShapeDtypeStruct((BLK, KVH * HD), BF),
        ],
        scratch_shapes=[
            pltpu.VMEM((5,) + unit, BF),
            pltpu.VMEM((4,) + unit, BF),
            pltpu.VMEM((2,) + unit, BF),
            pltpu.VMEM((3, 2, 128, KCOL), BF),
            pltpu.VMEM((2, 128, KCOL), BF),
            pltpu.VMEM((3, 2, 32, KCOL), BF),
            pltpu.VMEM((2, 32, KCOL), BF),
            pltpu.VMEM(unit, BF),
            pltpu.VMEM((2,) + unit, BF),
            pltpu.VMEM((2,) + unit, BF),
            pltpu.VMEM(unit, F32),
            pltpu.VMEM(unit, BF),
            pltpu.SemaphoreType.DMA((26,)),
            pltpu.SemaphoreType.DMA((6,)),
            pltpu.SemaphoreType.DMA((4,)),
            pltpu.SemaphoreType.DMA((3,)),
            pltpu.SemaphoreType.DMA((3,)),
            pltpu.SemaphoreType.DMA((8,)),
            pltpu.SemaphoreType.DMA((2,)),
            pltpu.SemaphoreType.DMA((6,)),
            pltpu.SemaphoreType.DMA((9,)),
        ],
        compiler_params=pltpu.CompilerParams(
            collective_id=1, has_side_effects=True, vmem_limit_bytes=32 * 1024 * 1024
        ),
        name="reduce",
    )(out, dq, g)


def on_device(queries, keys, values, grad_out, doc_lengths, share_prefix):
    q, do, kv = gather(queries, grad_out, keys, values)
    out, dq, g = attention(q, do, kv, doc_lengths, share_prefix)
    return tuple(reduce(out, dq, g))


def solution(mesh):
    rows = P(("ctx", "heads"), None)
    return jax.shard_map(
        on_device, mesh=mesh, in_specs=(rows, rows, rows, rows, P(), P()),
        out_specs=(rows, rows, rows, rows), check_vma=False,
    )
```

```python
import jax
import jax.numpy as jnp
from jax import lax
from jax.experimental import pallas as pl
from jax.experimental.pallas import tpu as pltpu
from jax.sharding import PartitionSpec as P

QH = 64
KVH = 8
HD = 128
PER = QH // KVH
DOCS = 16
MESH = pl.DeviceIdType.MESH
BF = jnp.bfloat16
F32 = jnp.float32

UNIT = 256
BLK = 64
BACK = 4
PRE = 1024
KEYS = PRE + (BACK + 1) * UNIT
GROUPS = 2
WIDE = PER * HD

ROWS = 128
LANES = PER * ROWS
SEEN = PRE + BACK * UNIT + ROWS
KC = 512
SCALE = HD ** (-0.5)
LOG2E = 1.4426950408889634
PART = 32
SEMS = 192
NT = (((1,), (1,)), ((), ()))


def kernel(
    lens, share, q_ref, do_ref, k_ref, v_ref, o_ref, odq_ref, dk_ref, dv_ref,
    q_in, do_in, kv, kt, s_scr, p_scr, q_scr, dot_scr, acc, m_scr, l_scr, gk, gv, out_buf, dq_buf,
    g_buf, core_buf, z_send, z_buf, x_send, x_buf, last_send, last_buf, w_send, w_buf, sum_buf, k_buf,
    send, recv, local,
):
    ctx = lax.axis_index("ctx")
    y = lax.axis_index("heads")
    core = ctx % 2
    slab = ctx // 2
    z = slab // 4
    x = slab % 4
    origin = z // 2
    source = (z == 0) & (x < 2)
    mine = pl.multiple_of(y * BLK, BLK)
    own = PRE + BACK * UNIT
    slot = [PRE + i * UNIT for i in range(BACK + 1)]

    def device(to_slab, to_core, to_y):
        return {"ctx": to_slab * 2 + to_core, "heads": to_y}

    sibling = device(slab, 1 - core, y)
    peers = [(y + 2) % 4, 3 - y, y + 1 - 2 * (y % 2)]

    @pl.when(slab < 2)
    def _():
        for g in range(GROUPS):
            kv[g, :, PRE:own, :] = jnp.zeros((2, BACK * UNIT, HD), BF)

    barrier = pltpu.get_barrier_semaphore()

    def greet(to):
        pl.semaphore_signal(barrier, inc=1, device_id=to, device_id_type=MESH)

    for step in range(1, 4):
        greet(device(slab, core, (y + step) % 4))
        greet(device(z * 4 + (x + step) % 4, core, y))
        greet(device((slab + 4 * step) % 16, core, y))
    for step in (1, 2, 14, 15):
        greet(device((slab + step) % 16, core, y))
    greet(sibling)

    @pl.when(source)
    def _():
        for i in range(8):
            @pl.when(8 * x + i != slab)
            def _():
                greet(device(8 * x + i, core, y))

    @pl.when(slab != origin)
    def _():
        greet(device(origin, core, y))

    pl.semaphore_wait(barrier, 14 + jnp.where(slab == 0, 7, jnp.where(slab == 1, 9, 1)))

    table = {}

    def number(name, count=1):
        if name not in table:
            table[name] = sum(c for _, c in table.values()), count
        return table[name][0]

    def remote(name, src, dst, to, shift=0, sent=None):
        at = number(name, 8 if name[0] == "home" else 1) + shift
        out = at if sent is None else number(sent)
        return pltpu.make_async_remote_copy(
            src_ref=src, dst_ref=dst, send_sem=send.at[out], recv_sem=recv.at[at],
            device_id=to, device_id_type=MESH,
        )


    def kv_head(g, i):
        n, ref = ((0, k_ref), (1, v_ref))[i // 4]
        to = (peers + [y])[i % 4]
        src = ref.at[:, pl.ds(pl.multiple_of((to * GROUPS + g) * HD, HD), HD)]
        dst = kv.at[g, n, pl.ds(own + mine, BLK), :]
        if i % 4 == 3:
            return pltpu.make_async_copy(src, dst, local.at[g * 2 + n])
        return remote(("kv", g, i), src, dst, device(slab, core, to))

    def q_head(g, i, n):
        ref, into = ((q_ref, q_in), (do_ref, do_in))[n]
        to = (peers + [y])[i]
        src = ref.at[:, pl.ds(pl.multiple_of((to * GROUPS + g) * WIDE, WIDE), WIDE)]
        dst = into.at[g, pl.ds(mine, BLK), :]
        if i == 3:
            return pltpu.make_async_copy(src, dst, local.at[4 + g * 2 + n])
        return remote(("q", g, i, n), src, dst, device(slab, core, to))

    def rows(g, at, count):
        return kv.at[g, :, pl.ds(at, count), :]

    def move(name, g, src, dst, count, to, sent=None):
        return remote((name, g), rows(g, src, count), rows(g, dst, count), to, sent=sent)

    piece = pl.multiple_of((core + 2 * origin) * UNIT + (slab % 8) * PART, PART)
    plane = pl.multiple_of((core + 2 * origin) * UNIT + (z % 2) * 4 * PART, 4 * PART)

    def scatter(g, i):
        return move(
            "piece", g, own + i * PART, pl.multiple_of((core + 2 * x) * UNIT + i * PART, PART), PART,
            device(8 * x + i, core, y), sent=("scatter", g, i),
        )

    def own_piece(g):
        return pltpu.make_async_copy(
            rows(g, own, PART), rows(g, pl.multiple_of(core * UNIT, PART), PART), local.at[8 + g]
        )

    def window(g, ahead):
        return move(
            ("window", ahead), g, own, slot[2] if ahead == 1 else slot[0], UNIT,
            device((slab + ahead) % 16, core, y),
        )

    def along_x(g, step):
        return move(("x", step), g, piece, piece, PART, device(z * 4 + (x + step) % 4, core, y))

    def along_z(g, step):
        return move(("z", step), g, plane, plane, 4 * PART, device((slab + 4 * step) % 16, core, y))

    def core_own(g):
        return move(("core", 3), g, own, slot[3], UNIT, sibling)

    def near_up(g):
        return move(("core", 1), g, slot[2], slot[1], UNIT, sibling)

    def near_down(g):
        return move(("core", 3), g, slot[2], slot[3], UNIT, sibling)

    def far_down(g):
        return move(("core", 1), g, slot[0], slot[1], UNIT, sibling)

    def half(g, i):
        at = pl.multiple_of((core + 2 * i) * UNIT, UNIT)
        return move(("half", i), g, at, at, UNIT, sibling)

    def kv_start(g):
        for i in range(8):
            kv_head(g, i).start()

    def q_start(g):
        for i in range(4):
            for n in range(2):
                q_head(g, i, n).start()

    def kv_stage1(g):
        for i in range(8):
            if i % 4 == 3:
                kv_head(g, i).wait()
            else:
                kv_head(g, i).wait_recv()

        @pl.when(source)
        def _():
            for i in range(8):
                @pl.when(8 * x + i != slab)
                def _():
                    scatter(g, i).start()

        @pl.when(slab == 0)
        def _():
            own_piece(g).start()

        for ahead in (1, 2):
            @pl.when(slab + ahead < 16)
            def _():
                window(g, ahead).start()

        @pl.when(core == 0)
        def _():
            core_own(g).start()

    def kv_stage2(g):
        @pl.when(slab == 0)
        def _():
            own_piece(g).wait()

        @pl.when(slab != 0)
        def _():
            move("piece", g, piece, piece, PART, sibling).wait_recv()

        for step in range(1, 4):
            along_x(g, step).start()

    def kv_stage3(g):
        for step in range(1, 4):
            along_x(g, step).wait_recv()
        for step in range(1, 4):
            along_z(g, step).start()

    def kv_stage4(g):
        for step in range(1, 4):
            along_z(g, step).wait_recv()
        for i in range(2):
            half(g, i).start()

    def kv_stage5(g):
        @pl.when(slab >= 1)
        def _():
            window(g, 1).wait_recv()

            @pl.when(core == 0)
            def _():
                near_up(g).start()

            @pl.when(core == 1)
            def _():
                near_down(g).start()

        @pl.when(slab >= 2)
        def _():
            window(g, 2).wait_recv()

            @pl.when(core == 1)
            def _():
                far_down(g).start()

    def kv_stage6(g):
        for i in range(2):
            half(g, i).wait_recv()

        @pl.when(core == 1)
        def _():
            core_own(g).wait_recv()

            @pl.when(slab >= 1)
            def _():
                near_up(g).wait_recv()

        @pl.when(core == 0)
        def _():
            @pl.when(slab >= 1)
            def _():
                near_down(g).wait_recv()

            @pl.when(slab >= 2)
            def _():
                far_down(g).wait_recv()


    def q_back(g, i, n):
        buf, ref = ((out_buf, o_ref), (dq_buf, odq_ref))[n]
        to = (peers + [y])[i]
        src = buf.at[g, pl.ds(pl.multiple_of(to * BLK, BLK), BLK), :]
        dst = ref.at[:, pl.ds(pl.multiple_of((y * GROUPS + g) * WIDE, WIDE), WIDE)]
        if i == 3:
            return pltpu.make_async_copy(src, dst, local.at[10 + g * 2 + n])
        return remote(("back", g, i, n), src, dst, device(slab, core, to))

    def g_rows(g, at, count):
        return g_buf.at[g, :, pl.ds(at, count), :]

    def core_sum(g, i):
        if i < 2:
            at = pl.multiple_of((1 - core + 2 * i) * UNIT, UNIT)
        else:
            at = slot[1 + 2 * (i - 2)]
        return remote(("csum", g, i), g_rows(g, at, UNIT), core_buf.at[g, i], sibling)

    def z_sum(g, step):
        to = (z + step) % 4
        at = pl.multiple_of((to % 2) * 4 * PART, 4 * PART)
        return remote(
            ("zsum", g, step), z_send.at[g, to // 2, :, pl.ds(at, 4 * PART), :], z_buf.at[g, step - 1],
            device((slab + 4 * step) % 16, core, y),
        )

    def x_sum(g, step):
        to = (x + step) % 4
        at = pl.multiple_of(to * PART, PART)
        return remote(
            ("xsum", g, step), x_send.at[g, :, pl.ds(at, PART), :], x_buf.at[g, step - 1],
            device(z * 4 + to, core, y),
        )

    def home(g):
        at = pl.multiple_of((slab % 8) * PART, PART)
        return remote(
            ("home", g), last_send.at[g], last_buf.at[g, :, pl.ds(at, PART), :], device(origin, core, y),
            shift=slab % 8, sent=("went", g),
        )

    def arrival(g, i):
        return remote(
            ("home", g), last_send.at[g], last_buf.at[g, :, pl.ds(i * PART, PART), :], sibling,
            shift=i, sent=("went", g),
        )

    def w_sum(g, back):
        return remote(
            ("wsum", g, back), w_send.at[g, back - 1], w_buf.at[g, back - 1],
            device((slab + 16 - back) % 16, core, y),
        )

    def k_back(g, i, n):
        ref = (dk_ref, dv_ref)[n]
        to = (peers + [y])[i]
        src = k_buf.at[g, n, pl.ds(pl.multiple_of(to * BLK, BLK), BLK), :]
        dst = ref.at[:, pl.ds(pl.multiple_of((y * GROUPS + g) * HD, HD), HD)]
        if i == 3:
            return pltpu.make_async_copy(src, dst, local.at[14 + g * 2 + n])
        return remote(("kback", g, i, n), src, dst, device(slab, core, to))

    def sum_stage1(g):
        g_buf[g, 0] = (gk[...] * SCALE).astype(BF)
        g_buf[g, 1] = gv[...].astype(BF)
        for i in range(4):
            core_sum(g, i).start()

    def sum_stage2(g):
        for i in range(2):
            core_sum(g, i).wait_recv()
            at = pl.multiple_of((core + 2 * i) * UNIT, UNIT)
            z_send[g, i] = (g_buf[g, :, pl.ds(at, UNIT), :].astype(F32) + core_buf[g, i].astype(F32)).astype(BF)
        for step in range(1, 4):
            z_sum(g, step).start()
        core_sum(g, 2).wait_recv()
        core_sum(g, 3).wait_recv()
        a = core_buf[g, 2].astype(F32)
        b = core_buf[g, 3].astype(F32)
        lower = core == 0
        far = g_buf[g, :, slot[0]:slot[0] + UNIT, :].astype(F32)
        near = g_buf[g, :, slot[2]:slot[2] + UNIT, :].astype(F32)
        here = g_buf[g, :, slot[4]:slot[4] + UNIT, :].astype(F32)
        w_send[g, 0] = (near + jnp.where(lower, a, b)).astype(BF)
        w_send[g, 1] = (far + jnp.where(lower, 0.0, a)).astype(BF)
        sum_buf[g] = here + jnp.where(lower, b, 0.0)
        for back in (1, 2):
            @pl.when(slab >= back)
            def _():
                w_sum(g, back).start()

    def sum_stage3(g):
        for step in range(1, 4):
            z_sum(g, step).wait_recv()
        at = pl.multiple_of((z % 2) * 4 * PART, 4 * PART)
        total = z_send[g, z // 2, :, pl.ds(at, 4 * PART), :].astype(F32)
        for i in range(3):
            total += z_buf[g, i].astype(F32)
        x_send[g] = total.astype(BF)
        for step in range(1, 4):
            x_sum(g, step).start()

    def sum_stage4(g):
        for step in range(1, 4):
            x_sum(g, step).wait_recv()
        total = x_send[g, :, pl.ds(pl.multiple_of(x * PART, PART), PART), :].astype(F32)
        for i in range(3):
            total += x_buf[g, i].astype(F32)
        last_send[g] = total.astype(BF)

        @pl.when(slab != origin)
        def _():
            home(g).start()

    def sum_stage5(g):
        for back in (1, 2):
            @pl.when(slab + back < 16)
            def _():
                w_sum(g, back).wait_recv()
                sum_buf[g] += w_buf[g, back - 1].astype(F32)

        @pl.when(source)
        def _():
            for i in range(8):
                @pl.when(8 * x + i != slab)
                def _():
                    arrival(g, i).wait_recv()

            @pl.when(slab == 0)
            def _():
                last_buf[g, :, 0:PART, :] = last_send[g]

            sum_buf[g] += last_buf[g].astype(F32)

        k_buf[g] = sum_buf[g].astype(BF)
        for i in range(4):
            for n in range(2):
                k_back(g, i, n).start()


    def hook(u, stage):
        g = u // 2
        if stage == 0:
            if u % 2 == 0:
                kv_stage6(g)
            for i in ((0, 1), (2, 3))[u % 2]:
                for n in range(2):
                    if i == 3:
                        q_head(g, i, n).wait()
                    else:
                        q_head(g, i, n).wait_recv()
        if stage == 2 or stage == 3:
            for i in ((0, 1), (2, 3))[u % 2]:
                q_back(g, i, stage - 2).start()
        if (u, stage) == (0, 1):
            kv_stage4(1)
            kv_stage5(1)
        if (u, stage) == (1, 3):
            sum_stage1(0)
        if (u, stage) == (2, 1):
            sum_stage2(0)
        if (u, stage) == (2, 3):
            sum_stage3(0)
        if (u, stage) == (3, 2):
            sum_stage4(0)
        if (u, stage) == (3, 3):
            sum_stage1(1)
            sum_stage5(0)
            sum_stage2(1)
            sum_stage3(1)
            sum_stage4(1)
            sum_stage5(1)

    def hooks(u, stage):
        for k in range(2 * GROUPS):
            @pl.when(u == k)
            def _():
                hook(k, stage)

    kv_start(0)
    kv_start(1)
    q_start(0)
    kv_stage1(0)
    kv_stage1(1)
    kv_stage2(0)
    kv_stage2(1)
    kv_stage3(0)
    kv_stage3(1)
    q_start(1)
    kv_stage4(0)
    kv_stage5(0)


    first = ctx * UNIT
    base = first - BACK * UNIT - PRE

    def unit(u, carry):
        g = u // 2
        late = y // 2
        r = jnp.where(u % 2 == 0, 1 - late, late)
        row_at = pl.multiple_of(r * ROWS, ROWS)
        w_at = pl.multiple_of(PRE + r * ROWS, ROWS)
        hooks(u, 0)

        @pl.when(u % 2 == 0)
        def _():
            for n in range(2):
                kt[n] = kv[g, n].astype(F32).T.astype(BF)
            gk[...] = jnp.zeros_like(gk)
            gv[...] = jnp.zeros_like(gv)

        pos = first + r * ROWS + lax.broadcasted_iota(jnp.int32, (1, LANES), 1) % ROWS
        start_i = jnp.zeros((1, LANES), jnp.int32)
        share_i = jnp.zeros((1, LANES), jnp.int32)
        begin = lens[0]
        for d in range(1, DOCS):
            inside = pos >= begin
            start_i = jnp.where(inside, begin, start_i)
            share_i = jnp.where(inside, share[d], share_i)
            begin = begin + lens[d]
        lim = jnp.where(share_i == 1, lens[0], 0)
        low = start_i - base - w_at
        high = pos - base - w_at

        blocks = []
        for at in range(0, PRE, KC):
            blocks.append((at, at, KC))
        for at in range(0, BACK * UNIT, KC):
            blocks.append((pl.multiple_of(w_at + at, ROWS), PRE + at, KC))
        blocks.append((pl.multiple_of(w_at + BACK * UNIT, ROWS), PRE + BACK * UNIT, ROWS))

        for h in range(PER):
            q_scr[h * ROWS:(h + 1) * ROWS, :] = q_in[g, pl.ds(row_at, ROWS), h * HD:(h + 1) * HD]
        top = jnp.full((8, LANES), -1e30, F32)
        for src, at, count in blocks:
            s = lax.dot_general(kv[g, 0, pl.ds(src, count), :], q_scr[...], NT, preferred_element_type=F32)
            j = lax.broadcasted_iota(jnp.int32, (count, LANES), 0)
            if at < PRE:
                ok = j < lim - at
            else:
                ok = j >= low - (at - PRE)
                if count == ROWS:
                    ok &= j <= high - (at - PRE)
            s = jnp.where(ok, s, -1e30)
            s_scr[at:at + count, :] = s
            top = jnp.maximum(top, jnp.max(s.reshape(count // 8, 8, LANES), axis=0))
        m_scr[...] = top
        hooks(u, 1)

        mc = jnp.max(m_scr[...], axis=0, keepdims=True) * (SCALE * LOG2E)
        total = jnp.zeros((8, LANES), F32)
        for src, at, count in blocks:
            p = jnp.exp2(s_scr[at:at + count, :] * (SCALE * LOG2E) - mc)
            total += jnp.sum(p.reshape(count // 8, 8, LANES), axis=0)
            pb = p.astype(BF)
            p_scr[at:at + count, :] = pb
            o = jnp.dot(kt[1, :, pl.ds(src, count)], pb, preferred_element_type=F32)
            if at == 0:
                acc[...] = o
            else:
                acc[...] += o
        inv = 1.0 / jnp.sum(total, axis=0, keepdims=True)
        out_t = acc[...] * inv
        out = out_t.T.astype(BF)
        parts = []
        for h in range(PER):
            out_buf[g, pl.ds(row_at, ROWS), h * HD:(h + 1) * HD] = out[h * ROWS:(h + 1) * ROWS, :]
            parts.append(do_in[g, pl.ds(row_at, ROWS), h * HD:(h + 1) * HD].astype(F32).T)
        do_t = (jnp.concatenate(parts, axis=1) * inv).astype(BF)
        dot_scr[...] = do_t
        l_scr[...] = jnp.sum(do_t.astype(F32) * out_t.astype(BF).astype(F32), axis=0, keepdims=True)
        hooks(u, 2)

        delta = l_scr[...]
        for src, at, count in blocks:
            dp = jnp.dot(kv[g, 1, pl.ds(src, count), :], dot_scr[...], preferred_element_type=F32)
            pb = p_scr[at:at + count, :]
            ds = (pb.astype(F32) * (dp - delta)).astype(BF)
            gv[pl.ds(src, count), :] += lax.dot_general(pb, dot_scr[...], NT, preferred_element_type=F32)
            gk[pl.ds(src, count), :] += jnp.dot(ds, q_scr[...], preferred_element_type=F32)
            o = jnp.dot(kt[0, :, pl.ds(src, count)], ds, preferred_element_type=F32)
            if at == 0:
                acc[...] = o
            else:
                acc[...] += o
        dq = (acc[...] * SCALE).T.astype(BF)
        for h in range(PER):
            dq_buf[g, pl.ds(row_at, ROWS), h * HD:(h + 1) * HD] = dq[h * ROWS:(h + 1) * ROWS, :]
        hooks(u, 3)
        return carry

    lax.fori_loop(0, 2 * GROUPS, unit, 0)


    for g in range(GROUPS):
        for n in range(2):
            for i in range(3):
                q_back(g, i, n).wait_recv()
                k_back(g, i, n).wait_recv()
            q_back(g, 3, n).wait()
            k_back(g, 3, n).wait()
        for n in range(2):
            for i in range(3):
                q_head(g, i, n).wait_send()
                kv_head(g, n * 4 + i).wait_send()
                q_back(g, i, n).wait_send()
                k_back(g, i, n).wait_send()
        for step in range(1, 4):
            along_x(g, step).wait_send()
            along_z(g, step).wait_send()
            z_sum(g, step).wait_send()
            x_sum(g, step).wait_send()
        for i in range(2):
            half(g, i).wait_send()
        for i in range(4):
            core_sum(g, i).wait_send()

        @pl.when(source)
        def _():
            for i in range(8):
                @pl.when(8 * x + i != slab)
                def _():
                    scatter(g, i).wait_send()

        for ahead in (1, 2):
            @pl.when(slab + ahead < 16)
            def _():
                window(g, ahead).wait_send()

            @pl.when(slab >= ahead)
            def _():
                w_sum(g, ahead).wait_send()

        @pl.when(core == 0)
        def _():
            core_own(g).wait_send()

            @pl.when(slab >= 1)
            def _():
                near_up(g).wait_send()

        @pl.when(core == 1)
        def _():
            @pl.when(slab >= 1)
            def _():
                near_down(g).wait_send()

            @pl.when(slab >= 2)
            def _():
                far_down(g).wait_send()

        @pl.when(slab != origin)
        def _():
            home(g).wait_send()

    assert sum(c for _, c in table.values()) <= SEMS


def on_device(queries, keys, values, grad_out, doc_lengths, share_prefix):
    anywhere = pl.BlockSpec(memory_space=pl.ANY)
    smem = pl.BlockSpec(memory_space=pltpu.SMEM)
    unit = (2, UNIT, HD)
    G = GROUPS
    return tuple(pl.pallas_call(
        kernel,
        in_specs=[smem, smem] + [anywhere] * 4,
        out_specs=[anywhere] * 4,
        out_shape=[
            jax.ShapeDtypeStruct((BLK, QH * HD), BF),
            jax.ShapeDtypeStruct((BLK, QH * HD), BF),
            jax.ShapeDtypeStruct((BLK, KVH * HD), BF),
            jax.ShapeDtypeStruct((BLK, KVH * HD), BF),
        ],
        scratch_shapes=[
            pltpu.VMEM((G, UNIT, WIDE), BF),
            pltpu.VMEM((G, UNIT, WIDE), BF),
            pltpu.VMEM((G, 2, KEYS, HD), BF),
            pltpu.VMEM((2, HD, KEYS), BF),
            pltpu.VMEM((SEEN, LANES), F32),
            pltpu.VMEM((SEEN, LANES), BF),
            pltpu.VMEM((LANES, HD), BF),
            pltpu.VMEM((HD, LANES), BF),
            pltpu.VMEM((HD, LANES), F32),
            pltpu.VMEM((8, LANES), F32),
            pltpu.VMEM((1, LANES), F32),
            pltpu.VMEM((KEYS, HD), F32),
            pltpu.VMEM((KEYS, HD), F32),
            pltpu.VMEM((G, UNIT, WIDE), BF),
            pltpu.VMEM((G, UNIT, WIDE), BF),
            pltpu.VMEM((G, 2, KEYS, HD), BF),
            pltpu.VMEM((G, 4) + unit, BF),
            pltpu.VMEM((G, 2) + unit, BF),
            pltpu.VMEM((G, 3, 2, 4 * PART, HD), BF),
            pltpu.VMEM((G, 2, 4 * PART, HD), BF),
            pltpu.VMEM((G, 3, 2, PART, HD), BF),
            pltpu.VMEM((G, 2, PART, HD), BF),
            pltpu.VMEM((G,) + unit, BF),
            pltpu.VMEM((G, 2) + unit, BF),
            pltpu.VMEM((G, 2) + unit, BF),
            pltpu.VMEM((G,) + unit, F32),
            pltpu.VMEM((G,) + unit, BF),
            pltpu.SemaphoreType.DMA((SEMS,)),
            pltpu.SemaphoreType.DMA((SEMS,)),
            pltpu.SemaphoreType.DMA((18,)),
        ],
        compiler_params=pltpu.CompilerParams(
            collective_id=0, has_side_effects=True, vmem_limit_bytes=60 * 1024 * 1024
        ),
        name="packed_attention",
    )(doc_lengths, share_prefix, queries, grad_out, keys, values))


def solution(mesh):
    rows = P(("ctx", "heads"), None)
    return jax.shard_map(
        on_device, mesh=mesh, in_specs=(rows, rows, rows, rows, P(), P()),
        out_specs=(rows, rows, rows, rows), check_vma=False,
    )
```

```python
import jax
import jax.numpy as jnp
from jax import lax
from jax.experimental import pallas as pl
from jax.experimental.pallas import tpu as pltpu
from jax.sharding import PartitionSpec as P

QH = 64
KVH = 8
HD = 128
PER = QH // KVH
DOCS = 16
MESH = pl.DeviceIdType.MESH
BF = jnp.bfloat16
F32 = jnp.float32

UNIT = 256
BLK = 64
BACK = 4
PRE = 1024
KEYS = PRE + (BACK + 1) * UNIT
GROUPS = 2
WIDE = PER * HD

ROWS = 128
LANES = PER * ROWS
KC = 512
SPAN = BACK * UNIT + ROWS
SCALE = HD ** (-0.5)
LOG2E = 1.4426950408889634
QUARTER = UNIT // 4
SEMS = 160
NT = (((1,), (1,)), ((), ()))


def kernel(
    lens, share, q_ref, do_ref, k_ref, v_ref, o_ref, odq_ref, dk_ref, dv_ref,
    q_in, do_in, kv, kt, s_scr, p_win, p_pre, q_scr, dot_scr, acc, out_t, do_t, dq_t, lim, stat, gk, gv,
    out_buf, dq_buf, g_buf, core_buf, z_send, z_buf, x_send, x_buf, last_send, last_buf, w_send, w_buf,
    sum_buf, k_buf, send, recv, local,
):
    ctx = lax.axis_index("ctx")
    y = lax.axis_index("heads")
    core = ctx % 2
    slab = ctx // 2
    z = slab // 4
    x = slab % 4
    mine = pl.multiple_of(y * BLK, BLK)
    own = PRE + BACK * UNIT
    slot = [PRE + i * UNIT for i in range(BACK + 1)]
    first = ctx * UNIT
    base = first - BACK * UNIT - PRE

    def device(to_slab, to_core, to_y):
        return {"ctx": to_slab * 2 + to_core, "heads": to_y}

    sibling = device(slab, 1 - core, y)
    peers = [y + 1 - 2 * (y % 2), 3 - y, (y + 2) % 4]
    halves = [y // 2, 1 - y // 2]
    of_half = ((0, 3), (1, 2))

    @pl.when(slab < 2)
    def _():
        for g in range(GROUPS):
            kv[g, :, PRE:own, :] = jnp.zeros((2, BACK * UNIT, HD), BF)

    barrier = pltpu.get_barrier_semaphore()

    def greet(to):
        pl.semaphore_signal(barrier, inc=1, device_id=to, device_id_type=MESH)

    for step in range(1, 4):
        greet(device(z * 4 + (x + step) % 4, core, y))
        greet(device((slab + 4 * step) % 16, core, y))
        greet(device(slab, core, (y + step) % 4))
    for step in (1, 2, 14, 15):
        greet(device((slab + step) % 16, core, y))
    greet(sibling)

    for h in range(2):
        pos = first + halves[h] * ROWS + lax.broadcasted_iota(jnp.int32, (1, LANES), 1) % ROWS
        start_i = jnp.zeros((1, LANES), jnp.int32)
        share_i = jnp.zeros((1, LANES), jnp.int32)
        begin = lens[0]
        for d in range(1, DOCS):
            inside = pos >= begin
            start_i = jnp.where(inside, begin, start_i)
            share_i = jnp.where(inside, share[d], share_i)
            begin = begin + lens[d]
        w_at = PRE + halves[h] * ROWS
        lim[h, 0:1, :] = jnp.where(share_i == 1, lens[0], 0)
        lim[h, 1:2, :] = start_i - base - w_at
        lim[h, 2:3, :] = pos - base - w_at

    pl.semaphore_wait(barrier, 14)

    table = {}

    def number(name):
        return table.setdefault(name, len(table))

    def remote(name, src, dst, to, sent=None):
        at = number(name)
        out = at if sent is None else number(sent)
        return pltpu.make_async_remote_copy(
            src_ref=src, dst_ref=dst, send_sem=send.at[out], recv_sem=recv.at[at],
            device_id=to, device_id_type=MESH,
        )


    def kv_head(g, i, n):
        ref = (k_ref, v_ref)[n]
        to = (peers + [y])[i]
        src = ref.at[:, pl.ds(pl.multiple_of((to * GROUPS + g) * HD, HD), HD)]
        dst = kv.at[g, n, pl.ds(own + mine, BLK), :]
        if i == 3:
            return pltpu.make_async_copy(src, dst, local.at[g * 2 + n])
        return remote(("kv", g, i, n), src, dst, device(slab, core, to))

    def q_head(g, i, n):
        ref, into = ((q_ref, q_in), (do_ref, do_in))[n]
        to = (peers + [y])[i]
        src = ref.at[:, pl.ds(pl.multiple_of((to * GROUPS + g) * WIDE, WIDE), WIDE)]
        dst = into.at[g, pl.ds(mine, BLK), :]
        if i == 3:
            return pltpu.make_async_copy(src, dst, local.at[4 + g * 2 + n])
        return remote(("q", g, i, n), src, dst, device(slab, core, to))

    def rows(g, at, count):
        return kv.at[g, :, pl.ds(at, count), :]

    def move(name, g, src, dst, count, to):
        return remote((name, g), rows(g, src, count), rows(g, dst, count), to)

    def unit_at(u):
        return pl.multiple_of((core + 2 * u) * UNIT, UNIT)

    def z_quarter(g, step):
        to = (z + step) % 4
        return remote(
            ("quarter", g, step), rows(g, pl.multiple_of(own + to * QUARTER, QUARTER), QUARTER),
            rows(g, pl.multiple_of(unit_at(x) + to * QUARTER, QUARTER), QUARTER),
            device((slab + 4 * step) % 16, core, y),
        )

    def own_quarter(g):
        return pltpu.make_async_copy(
            rows(g, own, QUARTER), rows(g, pl.multiple_of(unit_at(x), QUARTER), QUARTER), local.at[8 + g]
        )

    def quarter_at(u):
        return pl.multiple_of(unit_at(u) + z * QUARTER, QUARTER)

    def x_quarter(g, u, step):
        at = quarter_at(u)
        return remote(
            ("x", g, u, step), rows(g, at, QUARTER), rows(g, at, QUARTER), device(z * 4 + (u + step) % 4, core, y),
            sent=("xs", g, step),
        )

    def z_all(g, u, step):
        at = quarter_at(u)
        return move(("z", u, step), g, at, at, QUARTER, device((slab + 4 * step) % 16, core, y))

    def half_unit(g, u):
        return move(("half", u), g, unit_at(u), unit_at(u), UNIT, sibling)

    def window(g, ahead):
        return move(
            ("window", ahead), g, own, slot[2] if ahead == 1 else slot[0], UNIT,
            device((slab + ahead) % 16, core, y),
        )

    def core_own(g):
        return move(("core", 3), g, own, slot[3], UNIT, sibling)

    def near_up(g):
        return move(("core", 1), g, slot[2], slot[1], UNIT, sibling)

    def near_down(g):
        return move(("core", 3), g, slot[2], slot[3], UNIT, sibling)

    def far_down(g):
        return move(("core", 1), g, slot[0], slot[1], UNIT, sibling)

    def q_start(g, n):
        for i in (0, 3, 1, 2):
            q_head(g, i, n).start()

    def q_wait(g, n):
        for i in range(4):
            if i == 3:
                q_head(g, i, n).wait()
            else:
                q_head(g, i, n).wait_recv()

    def kv_start(g):
        for i in range(4):
            for n in range(2):
                kv_head(g, i, n).start()

    def kv_units(g):
        for n in range(2):
            for i in range(3):
                kv_head(g, i, n).wait_recv()
            kv_head(g, 3, n).wait()
        for ahead in (1, 2):
            @pl.when(slab + ahead < 16)
            def _():
                window(g, ahead).start()

        @pl.when(slab < 2)
        def _():
            for step in range(1, 4):
                z_quarter(g, step).start()
            own_quarter(g).start()

        @pl.when(core == 0)
        def _():
            core_own(g).start()

    def pre_x(g):
        @pl.when(slab < 2)
        def _():
            own_quarter(g).wait()

        for step in range(1, 4):
            @pl.when((x < 2) & (z == step))
            def _():
                z_quarter(g, step).wait_recv()

        for u in range(2):
            @pl.when(x == u)
            def _():
                for step in range(1, 4):
                    x_quarter(g, u, step).start()

    def pre_z(g):
        for u in range(2):
            for step in range(1, 4):
                @pl.when(x == (u + step) % 4)
                def _():
                    x_quarter(g, u, step).wait_recv()
        for u in range(2):
            for step in range(1, 4):
                z_all(g, u, step).start()

    def pre_core(g):
        for u in range(2):
            for step in range(1, 4):
                z_all(g, u, step).wait_recv()
            half_unit(g, u).start()

    def pre_done(g):
        for u in range(2):
            half_unit(g, u).wait_recv()

    def win_core(g):
        @pl.when(slab >= 1)
        def _():
            window(g, 1).wait_recv()

            @pl.when(core == 0)
            def _():
                near_up(g).start()

            @pl.when(core == 1)
            def _():
                near_down(g).start()

        @pl.when(slab >= 2)
        def _():
            window(g, 2).wait_recv()

            @pl.when(core == 1)
            def _():
                far_down(g).start()

    def win_done(g):
        @pl.when(core == 1)
        def _():
            core_own(g).wait_recv()

            @pl.when(slab >= 1)
            def _():
                near_up(g).wait_recv()

        @pl.when(core == 0)
        def _():
            @pl.when(slab >= 1)
            def _():
                near_down(g).wait_recv()

            @pl.when(slab >= 2)
            def _():
                far_down(g).wait_recv()


    def q_back(g, i, n):
        buf, ref = ((out_buf, o_ref), (dq_buf, odq_ref))[n]
        to = (peers + [y])[i]
        src = buf.at[g, pl.ds(pl.multiple_of(to * BLK, BLK), BLK), :]
        dst = ref.at[:, pl.ds(pl.multiple_of((y * GROUPS + g) * WIDE, WIDE), WIDE)]
        if i == 3:
            return pltpu.make_async_copy(src, dst, local.at[10 + g * 2 + n])
        return remote(("back", g, i, n), src, dst, device(slab, core, to))

    def core_sum(g, i):
        at = unit_at(i) + (1 - 2 * core) * UNIT if i < 2 else slot[1 + 2 * (i - 2)]
        if i < 2:
            at = pl.multiple_of(at, UNIT)
        return remote(("csum", g, i), g_buf.at[g, :, pl.ds(at, UNIT), :], core_buf.at[g, i], sibling)

    def z_sum(g, step):
        at = pl.multiple_of(((z + step) % 4) * QUARTER, QUARTER)
        return remote(
            ("zsum", g, step), z_send.at[g, :, :, pl.ds(at, QUARTER), :], z_buf.at[g, step - 1],
            device((slab + 4 * step) % 16, core, y),
        )

    def x_sum(g, u, step):
        return remote(
            ("xsum", g, u, step), x_send.at[g, u], x_buf.at[g, step - 1], device(z * 4 + u, core, y),
        )

    def home(g, step):
        at = pl.multiple_of(z * QUARTER, QUARTER)
        return remote(
            ("home", g, step), last_send.at[g], last_buf.at[g, :, pl.ds(at, QUARTER), :], device(x, core, y),
        )

    def w_sum(g, back):
        return remote(
            ("wsum", g, back), w_send.at[g, back - 1], w_buf.at[g, back - 1],
            device((slab + 16 - back) % 16, core, y),
        )

    def k_back(g, i, n):
        ref = (dk_ref, dv_ref)[n]
        to = (peers + [y])[i]
        src = k_buf.at[g, n, pl.ds(pl.multiple_of(to * BLK, BLK), BLK), :]
        dst = ref.at[:, pl.ds(pl.multiple_of((y * GROUPS + g) * HD, HD), HD)]
        if i == 3:
            return pltpu.make_async_copy(src, dst, local.at[14 + g * 2 + n])
        return remote(("kback", g, i, n), src, dst, device(slab, core, to))

    def pre_sum_core(g):
        for i in range(2):
            core_sum(g, i).start()

    def pre_sum_z(g):
        for i in range(2):
            core_sum(g, i).wait_recv()
            z_send[g, i] = (
                g_buf[g, :, pl.ds(unit_at(i), UNIT), :].astype(F32) + core_buf[g, i].astype(F32)
            ).astype(BF)
        for step in range(1, 4):
            z_sum(g, step).start()

    def pre_sum_x(g):
        for step in range(1, 4):
            z_sum(g, step).wait_recv()
        total = z_send[g, :, :, pl.ds(pl.multiple_of(z * QUARTER, QUARTER), QUARTER), :].astype(F32)
        for i in range(3):
            total += z_buf[g, i].astype(F32)
        x_send[g] = total.astype(BF)
        for u in range(2):
            for step in range(1, 4):
                @pl.when(x == (u + step) % 4)
                def _():
                    x_sum(g, u, step).start()

    def pre_sum_home(g):
        for u in range(2):
            @pl.when(x == u)
            def _():
                total = x_send[g, u].astype(F32)
                for step in range(1, 4):
                    x_sum(g, u, step).wait_recv()
                    total += x_buf[g, step - 1].astype(F32)
                last_send[g] = total.astype(BF)
                for step in range(1, 4):
                    @pl.when(z == step)
                    def _():
                        home(g, step).start()

    def win_sum_core(g):
        for i in (2, 3):
            core_sum(g, i).start()

    def win_sum_x(g):
        core_sum(g, 2).wait_recv()
        core_sum(g, 3).wait_recv()
        a = core_buf[g, 2].astype(F32)
        b = core_buf[g, 3].astype(F32)
        lower = core == 0
        far = g_buf[g, :, slot[0]:slot[0] + UNIT, :].astype(F32)
        near = g_buf[g, :, slot[2]:slot[2] + UNIT, :].astype(F32)
        here = g_buf[g, :, slot[4]:slot[4] + UNIT, :].astype(F32)
        w_send[g, 1] = (far + jnp.where(lower, 0.0, a)).astype(BF)
        w_send[g, 0] = (near + jnp.where(lower, a, b)).astype(BF)
        for back in (2, 1):
            @pl.when(slab >= back)
            def _():
                w_sum(g, back).start()
        sum_buf[g] = here + jnp.where(lower, b, 0.0)

    def sum_back(g):
        @pl.when(slab < 2)
        def _():
            for step in range(1, 4):
                home_at = step * QUARTER
                remote(
                    ("home", g, step), last_send.at[g], last_buf.at[g, :, pl.ds(home_at, QUARTER), :], sibling
                ).wait_recv()
            last_buf[g, :, 0:QUARTER, :] = last_send[g]
            sum_buf[g] += last_buf[g].astype(F32)

        for back in (1, 2):
            @pl.when(slab + back < 16)
            def _():
                w_sum(g, back).wait_recv()
                sum_buf[g] += w_buf[g, back - 1].astype(F32)

        k_buf[g] = sum_buf[g].astype(BF)
        for i in (2, 1, 0, 3):
            for n in range(2):
                k_back(g, i, n).start()


    def blocks_of(part, h):
        if part == 0:
            return [(at, at, KC) for at in range(0, PRE, KC)]
        w_at = PRE + halves[h] * ROWS
        blocks = [(pl.multiple_of(w_at + at, ROWS), at, KC) for at in range(0, BACK * UNIT, KC)]
        return blocks + [(pl.multiple_of(w_at + BACK * UNIT, ROWS), BACK * UNIT, ROWS)]

    def place(h):
        return pl.ds(pl.multiple_of(halves[h] * ROWS, ROWS), ROWS)

    def scores(g, h, part, state):
        state["top"] = jnp.full((8, LANES), -1e30, F32)

        def step(src, at, count):
            s = lax.dot_general(
                kv[g, 0, pl.ds(src, count), :], q_scr[g, h], NT, preferred_element_type=F32
            )
            j = lax.broadcasted_iota(jnp.int32, (count, LANES), 0)
            if part == 0:
                ok = j < lim[h, 0:1, :] - at
            else:
                ok = j >= lim[h, 1:2, :] - at
                if count == ROWS:
                    ok &= j <= lim[h, 2:3, :] - at
            s = jnp.where(ok, s, -1e30)
            s_scr[h, at:at + count, :] = s
            state["top"] = jnp.maximum(state["top"], jnp.max(s.reshape(count // 8, 8, LANES), axis=0))

        return [lambda b=b: step(*b) for b in blocks_of(part, h)]

    def weighted(g, h, part, state):
        p_scr = (p_pre, p_win)[part]

        def step(src, at, count):
            if at == 0:
                state["mc"] = jnp.max(state["top"], axis=0, keepdims=True) * (SCALE * LOG2E)
                state["sum"] = jnp.zeros((8, LANES), F32)
            p = jnp.exp2(s_scr[h, at:at + count, :] * (SCALE * LOG2E) - state["mc"])
            state["sum"] += jnp.sum(p.reshape(count // 8, 8, LANES), axis=0)
            pb = p.astype(BF)
            p_scr[g, h, at:at + count, :] = pb
            o = jnp.dot(kt[g, 1, :, pl.ds(src, count)], pb, preferred_element_type=F32)
            spot = acc.at[part, g, h]
            if at == 0:
                spot[...] = o
            else:
                spot[...] += o

        return [lambda b=b: step(*b) for b in blocks_of(part, h)]

    def turn(g, low, count):
        for n in range(2):
            kt[g, n, :, low:low + count] = kv[g, n, low:low + count, :].astype(F32).T.astype(BF)

    def both(g, part):
        state = [{}, {}]
        for step in scores(g, 0, part, state[0]):
            step()
        late = scores(g, 1, part, state[1])
        for step in weighted(g, 0, part, state[0]):
            late.pop(0)()
            step()
        for step in weighted(g, 1, part, state[1]):
            step()
        return state

    def window_forward(g):
        for h in range(2):
            for i in range(PER):
                q_scr[g, h, i * ROWS:(i + 1) * ROWS, :] = q_in[g, place(h), i * HD:(i + 1) * HD]
        turn(g, PRE, KEYS - PRE)
        state = both(g, 1)
        for h in range(2):
            stat[g, h, 0:1, :] = state[h]["mc"]
            stat[g, h, 1:2, :] = jnp.sum(state[h]["sum"], axis=0, keepdims=True)

    def prefix_forward(g):
        turn(g, 0, PRE)
        state = both(g, 0)
        for h in range(2):
            mw = stat[g, h, 0:1, :]
            lw = stat[g, h, 1:2, :]
            mp = state[h]["mc"]
            lp = jnp.sum(state[h]["sum"], axis=0, keepdims=True)
            m = jnp.maximum(mw, mp)
            aw = jnp.exp2(mw - m)
            ap = jnp.exp2(mp - m)
            inv = 1.0 / (aw * lw + ap * lp)
            fp = ap * inv
            fw = aw * inv
            stat[g, h, 0:1, :] = fp
            stat[g, h, 1:2, :] = fw
            o = acc[0, g, h] * fp + acc[1, g, h] * fw
            out_t[g, h] = o.astype(BF)
            out = o.T.astype(BF)
            for i in range(PER):
                out_buf[g, place(h), i * HD:(i + 1) * HD] = out[i * ROWS:(i + 1) * ROWS, :]

    def gradients(g, h, part):
        p_scr = (p_pre, p_win)[part]
        if part == 0:
            for i in range(PER):
                do_t[g, h, :, i * ROWS:(i + 1) * ROWS] = (
                    do_in[g, place(h), i * HD:(i + 1) * HD].astype(F32).T.astype(BF)
                )
        factor = stat[g, h, part:part + 1, :]
        scaled = (do_t[g, h].astype(F32) * factor).astype(BF)
        dot_scr[h] = scaled
        delta = jnp.sum(scaled.astype(F32) * out_t[g, h].astype(F32), axis=0, keepdims=True)
        first_half = h == (0 if part == 0 else 1)
        for src, at, count in blocks_of(part, h):
            dp = jnp.dot(kv[g, 1, pl.ds(src, count), :], dot_scr[h], preferred_element_type=F32)
            pb = p_scr[g, h, at:at + count, :]
            ds = (pb.astype(F32) * (dp - delta)).astype(BF)
            tv = lax.dot_general(pb, dot_scr[h], NT, preferred_element_type=F32)
            tk = jnp.dot(ds, q_scr[g, h], preferred_element_type=F32)
            if first_half:
                gv[pl.ds(src, count), :] = tv
                gk[pl.ds(src, count), :] = tk
            else:
                g_buf[g, 1, pl.ds(src, count), :] = (gv[pl.ds(src, count), :] + tv).astype(BF)
                g_buf[g, 0, pl.ds(src, count), :] = ((gk[pl.ds(src, count), :] + tk) * SCALE).astype(BF)
            o = jnp.dot(kt[g, 0, :, pl.ds(src, count)], ds, preferred_element_type=F32)
            spot = dq_t.at[g, h]
            if part == 0 and at == 0:
                spot[...] = o
            else:
                spot[...] += o

    def prefix_backward(g):
        for h in range(2):
            gradients(g, h, 0)

    def window_backward(g, h):
        apart = [pl.ds(pl.multiple_of(PRE + halves[1 - i] * SPAN, ROWS), ROWS) for i in range(2)]
        if h == 1:
            zero = jnp.zeros((ROWS, HD), F32)
            gk[apart[1], :] = zero
            gv[apart[1], :] = zero
        gradients(g, h, 1)
        if h == 0:
            g_buf[g, 1, apart[0], :] = gv[apart[0], :].astype(BF)
            g_buf[g, 0, apart[0], :] = (gk[apart[0], :] * SCALE).astype(BF)
        dq = (dq_t[g, h] * SCALE).T.astype(BF)
        for i in range(PER):
            dq_buf[g, place(h), i * HD:(i + 1) * HD] = dq[i * ROWS:(i + 1) * ROWS, :]


    def each_group(before, work, after):
        def body(g, carry):
            for k in range(GROUPS):
                @pl.when(g == k)
                def _():
                    before(k)
            work(g)
            for k in range(GROUPS):
                @pl.when(g == k)
                def _():
                    after(k)
            return carry

        lax.fori_loop(0, GROUPS, body, 0)

    kv_start(0)
    kv_start(1)
    q_start(0, 0)
    kv_units(0)
    kv_units(1)
    q_start(1, 0)
    pre_x(0)
    pre_x(1)
    q_start(0, 1)
    q_start(1, 1)
    pre_z(0)
    win_core(0)

    def before_wf(g):
        if g == 1:
            win_core(1)
        q_wait(g, 0)
        win_done(g)

    def after_wf(g):
        if g == 0:
            pre_z(1)
            pre_core(0)

    each_group(before_wf, window_forward, after_wf)

    def before_pf(g):
        if g == 0:
            pre_core(1)
        pre_done(g)

    def after_pf(g):
        for i in (1, 2, 0, 3):
            q_back(g, i, 0).start()

    each_group(before_pf, prefix_forward, after_pf)

    def before_pb(g):
        q_wait(g, 1)

    def after_pb(g):
        pre_sum_core(g)
        if g == 1:
            pre_sum_z(0)

    each_group(before_pb, prefix_backward, after_pb)

    def after_wb(g, h):
        for i in of_half[h]:
            q_back(g, i, 1).start()
        if (g, h) == (0, 1):
            pre_sum_z(1)
        if (g, h) == (0, 0):
            win_sum_core(0)
            pre_sum_x(0)
        if (g, h) == (1, 1):
            pre_sum_x(1)
            win_sum_x(0)
            pre_sum_home(0)
        if (g, h) == (1, 0):
            win_sum_core(1)
            pre_sum_home(1)
            win_sum_x(1)
            sum_back(0)
            sum_back(1)

    def wb_body(g, carry):
        for h in (1, 0):
            window_backward(g, h)
            for k in range(GROUPS):
                @pl.when(g == k)
                def _():
                    after_wb(k, h)
        return carry

    lax.fori_loop(0, GROUPS, wb_body, 0)


    for g in range(GROUPS):
        for n in range(2):
            for i in range(3):
                q_back(g, i, n).wait_recv()
                k_back(g, i, n).wait_recv()
            q_back(g, 3, n).wait()
            k_back(g, 3, n).wait()
        for n in range(2):
            for i in range(3):
                q_head(g, i, n).wait_send()
                kv_head(g, i, n).wait_send()
                q_back(g, i, n).wait_send()
                k_back(g, i, n).wait_send()
        for step in range(1, 4):
            z_sum(g, step).wait_send()
            for u in range(2):
                z_all(g, u, step).wait_send()

                @pl.when(x == u)
                def _():
                    x_quarter(g, u, step).wait_send()

                @pl.when(x == (u + step) % 4)
                def _():
                    x_sum(g, u, step).wait_send()

            @pl.when((x < 2) & (z == step))
            def _():
                home(g, step).wait_send()

            @pl.when(slab < 2)
            def _():
                z_quarter(g, step).wait_send()
        for u in range(2):
            half_unit(g, u).wait_send()
        for i in range(4):
            core_sum(g, i).wait_send()

        for ahead in (1, 2):
            @pl.when(slab + ahead < 16)
            def _():
                window(g, ahead).wait_send()

            @pl.when(slab >= ahead)
            def _():
                w_sum(g, ahead).wait_send()

        @pl.when(core == 0)
        def _():
            core_own(g).wait_send()

            @pl.when(slab >= 1)
            def _():
                near_up(g).wait_send()

        @pl.when(core == 1)
        def _():
            @pl.when(slab >= 1)
            def _():
                near_down(g).wait_send()

            @pl.when(slab >= 2)
            def _():
                far_down(g).wait_send()

    assert len(table) <= SEMS, len(table)


def on_device(queries, keys, values, grad_out, doc_lengths, share_prefix):
    anywhere = pl.BlockSpec(memory_space=pl.ANY)
    smem = pl.BlockSpec(memory_space=pltpu.SMEM)
    unit = (2, UNIT, HD)
    G = GROUPS
    return tuple(pl.pallas_call(
        kernel,
        in_specs=[smem, smem] + [anywhere] * 4,
        out_specs=[anywhere] * 4,
        out_shape=[
            jax.ShapeDtypeStruct((BLK, QH * HD), BF),
            jax.ShapeDtypeStruct((BLK, QH * HD), BF),
            jax.ShapeDtypeStruct((BLK, KVH * HD), BF),
            jax.ShapeDtypeStruct((BLK, KVH * HD), BF),
        ],
        scratch_shapes=[
            pltpu.VMEM((G, UNIT, WIDE), BF),
            pltpu.VMEM((G, UNIT, WIDE), BF),
            pltpu.VMEM((G, 2, KEYS, HD), BF),
            pltpu.VMEM((G, 2, HD, KEYS), BF),
            pltpu.VMEM((2, SPAN, LANES), F32),
            pltpu.VMEM((G, 2, SPAN, LANES), BF),
            pltpu.VMEM((G, 2, PRE, LANES), BF),
            pltpu.VMEM((G, 2, LANES, HD), BF),
            pltpu.VMEM((2, HD, LANES), BF),
            pltpu.VMEM((2, G, 2, HD, LANES), F32),
            pltpu.VMEM((G, 2, HD, LANES), BF),
            pltpu.VMEM((G, 2, HD, LANES), BF),
            pltpu.VMEM((G, 2, HD, LANES), F32),
            pltpu.VMEM((2, 8, LANES), jnp.int32),
            pltpu.VMEM((G, 2, 8, LANES), F32),
            pltpu.VMEM((KEYS, HD), F32),
            pltpu.VMEM((KEYS, HD), F32),
            pltpu.VMEM((G, UNIT, WIDE), BF),
            pltpu.VMEM((G, UNIT, WIDE), BF),
            pltpu.VMEM((G, 2, KEYS, HD), BF),
            pltpu.VMEM((G, 4) + unit, BF),
            pltpu.VMEM((G, 2) + unit, BF),
            pltpu.VMEM((G, 3, 2, 2, QUARTER, HD), BF),
            pltpu.VMEM((G, 2, 2, QUARTER, HD), BF),
            pltpu.VMEM((G, 3, 2, QUARTER, HD), BF),
            pltpu.VMEM((G, 2, QUARTER, HD), BF),
            pltpu.VMEM((G,) + unit, BF),
            pltpu.VMEM((G, 2) + unit, BF),
            pltpu.VMEM((G, 2) + unit, BF),
            pltpu.VMEM((G,) + unit, F32),
            pltpu.VMEM((G,) + unit, BF),
            pltpu.SemaphoreType.DMA((SEMS,)),
            pltpu.SemaphoreType.DMA((SEMS,)),
            pltpu.SemaphoreType.DMA((18,)),
        ],
        compiler_params=pltpu.CompilerParams(
            collective_id=0, has_side_effects=True, vmem_limit_bytes=60 * 1024 * 1024
        ),
        name="packed_attention",
    )(doc_lengths, share_prefix, queries, grad_out, keys, values))


def solution(mesh):
    rows = P(("ctx", "heads"), None)
    return jax.shard_map(
        on_device, mesh=mesh, in_specs=(rows, rows, rows, rows, P(), P()),
        out_specs=(rows, rows, rows, rows), check_vma=False,
    )
```

```python
import jax
import jax.numpy as jnp
from jax import lax
from jax.experimental import pallas as pl
from jax.experimental.pallas import tpu as pltpu
from jax.sharding import PartitionSpec as P

QH = 64
KVH = 8
HD = 128
PER = QH // KVH
DOCS = 16
MESH = pl.DeviceIdType.MESH
BF = jnp.bfloat16
F32 = jnp.float32

UNIT = 256
BLK = 64
BACK = 4
PRE = 1024
KEYS = PRE + (BACK + 1) * UNIT
GROUPS = 2
WIDE = PER * HD

ROWS = 128
LANES = PER * ROWS
KC = 512
SPAN = BACK * UNIT + ROWS
SCALE = HD ** (-0.5)
LOG2E = 1.4426950408889634
QUARTER = UNIT // 4
SENDS, ARRIVALS = 49, 59
NT = (((1,), (1,)), ((), ()))


def kernel(
    lens, share, q_ref, do_ref, k_ref, v_ref, o_ref, odq_ref, dk_ref, dv_ref,
    q_in, do_in, kv, kt, s_scr, p_win, p_pre, q_scr, dot_scr, acc, out_t, do_t, lim, stat, gk, gv,
    out_buf, dq_buf, g_buf, core_buf, z_send, z_buf, x_send, x_buf, last_send, last_buf, w_send, w_buf,
    sum_buf, k_buf, send, recv, local,
):
    ctx = lax.axis_index("ctx")
    y = lax.axis_index("heads")
    core = ctx % 2
    slab = ctx // 2
    z = slab // 4
    x = slab % 4
    mine = pl.multiple_of(y * BLK, BLK)
    own = PRE + BACK * UNIT
    slot = [PRE + i * UNIT for i in range(BACK + 1)]
    first = ctx * UNIT
    base = first - BACK * UNIT - PRE

    def device(to_slab, to_core, to_y):
        return {"ctx": to_slab * 2 + to_core, "heads": to_y}

    sibling = device(slab, 1 - core, y)
    peers = [y + 1 - 2 * (y % 2), 3 - y, (y + 2) % 4]
    halves = [y // 2, 1 - y // 2]
    of_half = ((0, 3), (1, 2))

    @pl.when(slab < 2)
    def _():
        for g in range(GROUPS):
            kv[g, :, PRE:own, :] = jnp.zeros((2, BACK * UNIT, HD), BF)

    barrier = pltpu.get_barrier_semaphore()

    def greet(to):
        pl.semaphore_signal(barrier, inc=1, device_id=to, device_id_type=MESH)

    for step in range(1, 4):
        greet(device(z * 4 + (x + step) % 4, core, y))
        greet(device((slab + 4 * step) % 16, core, y))
        greet(device(slab, core, (y + step) % 4))
    for step in (1, 2, 14, 15):
        greet(device((slab + step) % 16, core, y))
    greet(sibling)
    source = slab < 2
    spreads = x < 2
    alone = (z == 0) & (y == 0)

    @pl.when(source)
    def _():
        for step in range(4):
            @pl.when(jnp.logical_not(alone) | (step > 0))
            def _():
                greet(device(y * 4 + x, core, (y + step) % 4))

    @pl.when(spreads & jnp.logical_not(alone))
    def _():
        greet(device(x, core, z))

    for h in range(2):
        pos = first + halves[h] * ROWS + lax.broadcasted_iota(jnp.int32, (1, LANES), 1) % ROWS
        start_i = jnp.zeros((1, LANES), jnp.int32)
        share_i = jnp.zeros((1, LANES), jnp.int32)
        begin = lens[0]
        for d in range(1, DOCS):
            inside = pos >= begin
            start_i = jnp.where(inside, begin, start_i)
            share_i = jnp.where(inside, share[d], share_i)
            begin = begin + lens[d]
        w_at = PRE + halves[h] * ROWS
        lim[h, 0:1, :] = jnp.where(share_i == 1, lens[0], 0)
        lim[h, 1:2, :] = start_i - base - w_at
        lim[h, 2:3, :] = pos - base - w_at

    one = jnp.where(alone, 1, 0)
    pl.semaphore_wait(barrier, 14 + jnp.where(source, 4 - one, 0) + jnp.where(spreads, 1 - one, 0))

    sends, arrivals = {}, {}

    def remote(name, src, dst, to, sent=None):
        at = arrivals.setdefault(name, len(arrivals))
        out = sends.setdefault(name if sent is None else sent, len(sends))
        return pltpu.make_async_remote_copy(
            src_ref=src, dst_ref=dst, send_sem=send.at[out], recv_sem=recv.at[at],
            device_id=to, device_id_type=MESH,
        )

    def arrived(name, size):
        pltpu.make_async_copy(size, size, recv.at[arrivals[name]]).wait()

    def left(name, size):
        pltpu.make_async_copy(size, size, send.at[sends[name]]).wait()

    def size_of(count):
        return kv.at[0, 0, 0:count, :]


    def columns(ref, to, g):
        return ref.at[:, pl.ds(pl.multiple_of((to * GROUPS + g) * HD, HD), HD)]

    def kv_head(g, i, n):
        ref = (k_ref, v_ref)[n]
        to = (peers + [y])[i]
        src = ref.at[:, pl.ds(pl.multiple_of((to * GROUPS + g) * HD, HD), HD)]
        dst = kv.at[g, n, pl.ds(own + mine, BLK), :]
        if i == 3:
            return pltpu.make_async_copy(src, dst, local.at[g * 2 + n])
        return remote(("kv", g), src, dst, device(slab, core, to))

    def q_head(g, i, n):
        ref, into = ((q_ref, q_in), (do_ref, do_in))[n]
        to = (peers + [y])[i]
        src = ref.at[:, pl.ds(pl.multiple_of((to * GROUPS + g) * WIDE, WIDE), WIDE)]
        dst = into.at[g, pl.ds(mine, BLK), :]
        if i == 3:
            return pltpu.make_async_copy(src, dst, local.at[4 + g * 2 + n])
        return remote(("q", g, n), src, dst, device(slab, core, to))

    def rows(g, at, count):
        return kv.at[g, :, pl.ds(at, count), :]

    def move(name, g, src, dst, count, to):
        return remote((name, g), rows(g, src, count), rows(g, dst, count), to)

    def unit_at(u):
        return pl.multiple_of((core + 2 * u) * UNIT, UNIT)

    def spread_in(g, step, n):
        src = columns((k_ref, v_ref)[n], (y + step) % 4, g)
        dst = kv.at[g, n, pl.ds(pl.multiple_of(unit_at(x) + mine, BLK), BLK), :]
        return remote(
            ("in",), src, dst, device(y * 4 + x, core, (y + step) % 4), sent=("ins", step > 0)
        )

    def spread_own(g, n):
        src = columns((k_ref, v_ref)[n], y, g)
        return pltpu.make_async_copy(
            src, kv.at[g, n, pl.ds(pl.multiple_of(unit_at(x) + mine, BLK), BLK), :], local.at[18 + g * 2 + n]
        )

    def quarter(u):
        return kv.at[:, :, pl.ds(pl.multiple_of(unit_at(u) + z * QUARTER, QUARTER), QUARTER), :]

    def along_x(u, step):
        return remote(
            ("x", u, step), quarter(u), quarter(u), device(z * 4 + (u + step) % 4, core, y), sent=("xs",)
        )

    def along_z(g, u, step):
        at = pl.multiple_of(unit_at(u) + z * QUARTER, QUARTER)
        return move("z", g, at, at, QUARTER, device((slab + 4 * step) % 16, core, y))

    def half_unit(g, u):
        return move(("half", u), g, unit_at(u), unit_at(u), UNIT, sibling)

    def window(g, ahead):
        return move(
            ("window", ahead), g, own, slot[2] if ahead == 1 else slot[0], UNIT,
            device((slab + ahead) % 16, core, y),
        )

    def core_own(g):
        return move(("core", 3), g, own, slot[3], UNIT, sibling)

    def near_up(g):
        return move(("core", 1), g, slot[2], slot[1], UNIT, sibling)

    def near_down(g):
        return move(("core", 3), g, slot[2], slot[3], UNIT, sibling)

    def far_down(g):
        return move(("core", 1), g, slot[0], slot[1], UNIT, sibling)

    def q_start(g, n):
        for i in (0, 3, 1, 2):
            q_head(g, i, n).start()

    def q_wait(g, n):
        arrived(("q", g, n), q_in.at[g, 0:3 * BLK, :])
        q_head(g, 3, n).wait()

    def kv_start(g):
        for i in range(4):
            for n in range(2):
                kv_head(g, i, n).start()

    def kv_units(g):
        arrived(("kv", g), size_of(6 * BLK))
        for n in range(2):
            kv_head(g, 3, n).wait()
        for ahead in (1, 2):
            @pl.when(slab + ahead < 16)
            def _():
                window(g, ahead).start()

        @pl.when(core == 0)
        def _():
            core_own(g).start()

    def pre_in():
        @pl.when(source)
        def _():
            for g in range(GROUPS):
                for n in range(2):
                    @pl.when(jnp.logical_not(alone))
                    def _():
                        spread_in(g, 0, n).start()

                    @pl.when(alone)
                    def _():
                        spread_own(g, n).start()

                    for step in range(1, 4):
                        spread_in(g, step, n).start()

    def pre_x():
        for u in range(2):
            @pl.when(x == u)
            def _():
                @pl.when(jnp.logical_not(alone))
                def _():
                    arrived(("in",), size_of(4 * BLK))

                @pl.when(alone)
                def _():
                    for g in range(GROUPS):
                        for n in range(2):
                            spread_own(g, n).wait()

                for step in (2, 1, 3):
                    along_x(u, step).start()

    def pre_z():
        for u in range(2):
            for step in range(1, 4):
                @pl.when(x == (u + step) % 4)
                def _():
                    along_x(u, step).wait_recv()
        for g in range(GROUPS):
            for step in (2, 1, 3):
                for u in range(2):
                    along_z(g, u, step).start()

    def pre_core(g):
        arrived(("z", g), size_of(12 * QUARTER))
        for u in range(2):
            half_unit(g, u).start()

    def pre_done(g):
        for u in range(2):
            half_unit(g, u).wait_recv()

    def win_core(g):
        @pl.when(slab >= 1)
        def _():
            window(g, 1).wait_recv()

            @pl.when(core == 0)
            def _():
                near_up(g).start()

            @pl.when(core == 1)
            def _():
                near_down(g).start()

        @pl.when(slab >= 2)
        def _():
            window(g, 2).wait_recv()

            @pl.when(core == 1)
            def _():
                far_down(g).start()

    def win_done(g):
        @pl.when(core == 1)
        def _():
            core_own(g).wait_recv()

            @pl.when(slab >= 1)
            def _():
                near_up(g).wait_recv()

        @pl.when(core == 0)
        def _():
            @pl.when(slab >= 1)
            def _():
                near_down(g).wait_recv()

            @pl.when(slab >= 2)
            def _():
                far_down(g).wait_recv()


    def q_back(g, i, n):
        buf, ref = ((out_buf, o_ref), (dq_buf, odq_ref))[n]
        to = (peers + [y])[i]
        src = buf.at[g, pl.ds(pl.multiple_of(to * BLK, BLK), BLK), :]
        dst = ref.at[:, pl.ds(pl.multiple_of((y * GROUPS + g) * WIDE, WIDE), WIDE)]
        if i == 3:
            return pltpu.make_async_copy(src, dst, local.at[10 + g * 2 + n])
        return remote(("back", g, n), src, dst, device(slab, core, to))

    def core_sum(g, i):
        at = unit_at(i) + (1 - 2 * core) * UNIT if i < 2 else slot[1 + 2 * (i - 2)]
        if i < 2:
            at = pl.multiple_of(at, UNIT)
        return remote(("csum", g, i), g_buf.at[g, :, pl.ds(at, UNIT), :], core_buf.at[g, i], sibling)

    def z_sum(g, step):
        at = pl.multiple_of(((z + step) % 4) * QUARTER, QUARTER)
        return remote(
            ("zsum", g), z_send.at[g, :, :, pl.ds(at, QUARTER), :], z_buf.at[g, step - 1],
            device((slab + 4 * step) % 16, core, y),
        )

    def x_sum(g, u, step):
        return remote(
            ("xsum", g, step), x_send.at[g, u], x_buf.at[g, step - 1], device(z * 4 + u, core, y),
            sent=("xsums", g, u),
        )

    def home(g, step):
        at = pl.multiple_of(z * QUARTER, QUARTER)
        return remote(
            ("home", g, step), last_send.at[g], last_buf.at[g, :, pl.ds(at, QUARTER), :], device(x, core, y),
            sent=("homes", g),
        )

    def w_sum(g, back):
        return remote(
            ("wsum", g, back), w_send.at[g, back - 1], w_buf.at[g, back - 1],
            device((slab + 16 - back) % 16, core, y),
        )

    def k_back(g, i, n):
        ref = (dk_ref, dv_ref)[n]
        to = (peers + [y])[i]
        src = k_buf.at[g, n, pl.ds(pl.multiple_of(to * BLK, BLK), BLK), :]
        dst = ref.at[:, pl.ds(pl.multiple_of((y * GROUPS + g) * HD, HD), HD)]
        if i == 3:
            return pltpu.make_async_copy(src, dst, local.at[14 + g * 2 + n])
        return remote(("kback", g), src, dst, device(slab, core, to))

    def pre_sum_core(g):
        for i in range(2):
            core_sum(g, i).start()

    def pre_sum_z(g):
        for i in range(2):
            core_sum(g, i).wait_recv()
            z_send[g, i] = (
                g_buf[g, :, pl.ds(unit_at(i), UNIT), :].astype(F32) + core_buf[g, i].astype(F32)
            ).astype(BF)
        for step in range(1, 4):
            z_sum(g, step).start()

    def pre_sum_x(g):
        arrived(("zsum", g), z_buf.at[g])
        total = z_send[g, :, :, pl.ds(pl.multiple_of(z * QUARTER, QUARTER), QUARTER), :].astype(F32)
        for i in range(3):
            total += z_buf[g, i].astype(F32)
        x_send[g] = total.astype(BF)
        for u in range(2):
            for step in range(1, 4):
                @pl.when(x == (u + step) % 4)
                def _():
                    x_sum(g, u, step).start()

    def pre_sum_home(g):
        for u in range(2):
            @pl.when(x == u)
            def _():
                total = x_send[g, u].astype(F32)
                for step in range(1, 4):
                    x_sum(g, u, step).wait_recv()
                    total += x_buf[g, step - 1].astype(F32)
                last_send[g] = total.astype(BF)
                for step in range(1, 4):
                    @pl.when(z == step)
                    def _():
                        home(g, step).start()

    def win_sum_core(g):
        for i in (2, 3):
            core_sum(g, i).start()

    def win_sum_x(g):
        core_sum(g, 2).wait_recv()
        core_sum(g, 3).wait_recv()
        a = core_buf[g, 2].astype(F32)
        b = core_buf[g, 3].astype(F32)
        lower = core == 0
        far = g_buf[g, :, slot[0]:slot[0] + UNIT, :].astype(F32)
        near = g_buf[g, :, slot[2]:slot[2] + UNIT, :].astype(F32)
        here = g_buf[g, :, slot[4]:slot[4] + UNIT, :].astype(F32)
        w_send[g, 1] = (far + jnp.where(lower, 0.0, a)).astype(BF)
        w_send[g, 0] = (near + jnp.where(lower, a, b)).astype(BF)
        for back in (2, 1):
            @pl.when(slab >= back)
            def _():
                w_sum(g, back).start()
        sum_buf[g] = here + jnp.where(lower, b, 0.0)

    def sum_back(g):
        @pl.when(slab < 2)
        def _():
            for step in range(1, 4):
                home_at = step * QUARTER
                remote(
                    ("home", g, step), last_send.at[g], last_buf.at[g, :, pl.ds(home_at, QUARTER), :], sibling,
                    sent=("homes", g),
                ).wait_recv()
            last_buf[g, :, 0:QUARTER, :] = last_send[g]
            sum_buf[g] += last_buf[g].astype(F32)

        for back in (1, 2):
            @pl.when(slab + back < 16)
            def _():
                w_sum(g, back).wait_recv()
                sum_buf[g] += w_buf[g, back - 1].astype(F32)

        k_buf[g] = sum_buf[g].astype(BF)
        for i in (2, 1, 0, 3):
            for n in range(2):
                k_back(g, i, n).start()


    def blocks_of(part, h):
        if part == 0:
            return [(at, at, KC) for at in range(0, PRE, KC)]
        w_at = PRE + halves[h] * ROWS
        blocks = [(pl.multiple_of(w_at + at, ROWS), at, KC) for at in range(0, BACK * UNIT, KC)]
        return blocks + [(pl.multiple_of(w_at + BACK * UNIT, ROWS), BACK * UNIT, ROWS)]

    def place(h):
        return pl.ds(pl.multiple_of(halves[h] * ROWS, ROWS), ROWS)

    def scores(g, h, part, state):
        state["top"] = jnp.full((8, LANES), -1e30, F32)

        def step(src, at, count):
            s = lax.dot_general(
                kv[g, 0, pl.ds(src, count), :], q_scr[g, h], NT, preferred_element_type=F32
            )
            j = lax.broadcasted_iota(jnp.int32, (count, LANES), 0)
            if part == 0:
                ok = j < lim[h, 0:1, :] - at
            else:
                ok = j >= lim[h, 1:2, :] - at
                if count == ROWS:
                    ok &= j <= lim[h, 2:3, :] - at
            s = jnp.where(ok, s, -1e30)
            s_scr[h, at:at + count, :] = s
            state["top"] = jnp.maximum(state["top"], jnp.max(s.reshape(count // 8, 8, LANES), axis=0))

        return [lambda b=b: step(*b) for b in blocks_of(part, h)]

    def weighted(g, h, part, state):
        p_scr = (p_pre, p_win)[part]

        def step(src, at, count):
            if at == 0:
                state["mc"] = jnp.max(state["top"], axis=0, keepdims=True) * (SCALE * LOG2E)
                state["sum"] = jnp.zeros((8, LANES), F32)
            p = jnp.exp2(s_scr[h, at:at + count, :] * (SCALE * LOG2E) - state["mc"])
            state["sum"] += jnp.sum(p.reshape(count // 8, 8, LANES), axis=0)
            pb = p.astype(BF)
            p_scr[g, h, at:at + count, :] = pb
            o = jnp.dot(kt[g, 1, :, pl.ds(src, count)], pb, preferred_element_type=F32)
            spot = acc.at[part, g, h]
            if at == 0:
                spot[...] = o
            else:
                spot[...] += o

        return [lambda b=b: step(*b) for b in blocks_of(part, h)]

    def turn(g, low, count):
        for n in range(2):
            kt[g, n, :, low:low + count] = kv[g, n, low:low + count, :].astype(F32).T.astype(BF)

    def both(g, part):
        state = [{}, {}]
        for step in scores(g, 0, part, state[0]):
            step()
        late = scores(g, 1, part, state[1])
        for step in weighted(g, 0, part, state[0]):
            late.pop(0)()
            step()
        for step in weighted(g, 1, part, state[1]):
            step()
        return state

    def window_forward(g):
        for h in range(2):
            for i in range(PER):
                q_scr[g, h, i * ROWS:(i + 1) * ROWS, :] = q_in[g, place(h), i * HD:(i + 1) * HD]
        turn(g, PRE, KEYS - PRE)
        state = both(g, 1)
        for h in range(2):
            stat[g, h, 0:1, :] = state[h]["mc"]
            stat[g, h, 1:2, :] = jnp.sum(state[h]["sum"], axis=0, keepdims=True)

    def prefix_forward(g):
        turn(g, 0, PRE)
        state = both(g, 0)
        for h in range(2):
            mw = stat[g, h, 0:1, :]
            lw = stat[g, h, 1:2, :]
            mp = state[h]["mc"]
            lp = jnp.sum(state[h]["sum"], axis=0, keepdims=True)
            m = jnp.maximum(mw, mp)
            aw = jnp.exp2(mw - m)
            ap = jnp.exp2(mp - m)
            inv = 1.0 / (aw * lw + ap * lp)
            fp = ap * inv
            fw = aw * inv
            stat[g, h, 0:1, :] = fp
            stat[g, h, 1:2, :] = fw
            o = acc[0, g, h] * fp + acc[1, g, h] * fw
            out_t[g, h] = o.astype(BF)
            out = o.T.astype(BF)
            for i in range(PER):
                out_buf[g, place(h), i * HD:(i + 1) * HD] = out[i * ROWS:(i + 1) * ROWS, :]

    def gradients(g, h, part):
        p_scr = (p_pre, p_win)[part]
        if part == 0:
            for i in range(PER):
                do_t[g, h, :, i * ROWS:(i + 1) * ROWS] = (
                    do_in[g, place(h), i * HD:(i + 1) * HD].astype(F32).T.astype(BF)
                )
        factor = stat[g, h, part:part + 1, :]
        scaled = (do_t[g, h].astype(F32) * factor).astype(BF)
        dot_scr[h] = scaled
        delta = jnp.sum(scaled.astype(F32) * out_t[g, h].astype(F32), axis=0, keepdims=True)
        first_half = h == (0 if part == 0 else 1)
        for src, at, count in blocks_of(part, h):
            dp = jnp.dot(kv[g, 1, pl.ds(src, count), :], dot_scr[h], preferred_element_type=F32)
            pb = p_scr[g, h, at:at + count, :]
            ds = (pb.astype(F32) * (dp - delta)).astype(BF)
            tv = lax.dot_general(pb, dot_scr[h], NT, preferred_element_type=F32)
            tk = jnp.dot(ds, q_scr[g, h], preferred_element_type=F32)
            if first_half:
                gv[pl.ds(src, count), :] = tv
                gk[pl.ds(src, count), :] = tk
            else:
                g_buf[g, 1, pl.ds(src, count), :] = (gv[pl.ds(src, count), :] + tv).astype(BF)
                g_buf[g, 0, pl.ds(src, count), :] = ((gk[pl.ds(src, count), :] + tk) * SCALE).astype(BF)
            p_scr[g, h, at:at + count, :] = ds

    def window_backward(g, h):
        apart = [pl.ds(pl.multiple_of(PRE + halves[1 - i] * SPAN, ROWS), ROWS) for i in range(2)]
        if h == 1:
            zero = jnp.zeros((ROWS, HD), F32)
            gk[apart[1], :] = zero
            gv[apart[1], :] = zero
        gradients(g, h, 1)
        if h == 0:
            g_buf[g, 1, apart[0], :] = gv[apart[0], :].astype(BF)
            g_buf[g, 0, apart[0], :] = (gk[apart[0], :] * SCALE).astype(BF)

    def query_gradients(g, h):
        w_at = pl.multiple_of(PRE + halves[h] * ROWS, ROWS)
        o = jnp.dot(kt[g, 0, :, 0:PRE], p_pre[g, h], preferred_element_type=F32)
        o += jnp.dot(kt[g, 0, :, pl.ds(w_at, SPAN)], p_win[g, h], preferred_element_type=F32)
        dq = (o * SCALE).T.astype(BF)
        for i in range(PER):
            dq_buf[g, place(h), i * HD:(i + 1) * HD] = dq[i * ROWS:(i + 1) * ROWS, :]


    def each_group(before, work, after):
        def body(g, carry):
            for k in range(GROUPS):
                @pl.when(g == k)
                def _():
                    before(k)
            work(g)
            for k in range(GROUPS):
                @pl.when(g == k)
                def _():
                    after(k)
            return carry

        lax.fori_loop(0, GROUPS, body, 0)

    pre_in()
    kv_start(0)
    kv_start(1)
    q_start(0, 0)
    pre_x()
    kv_units(0)
    kv_units(1)
    q_start(1, 0)
    pre_z()
    q_start(0, 1)
    q_start(1, 1)
    win_core(0)

    def before_wf(g):
        if g == 1:
            win_core(1)
        q_wait(g, 0)
        win_done(g)

    def after_wf(g):
        if g == 0:
            pre_core(0)

    each_group(before_wf, window_forward, after_wf)

    def before_pf(g):
        if g == 0:
            pre_core(1)
        pre_done(g)

    def after_pf(g):
        for i in (1, 2, 0, 3):
            q_back(g, i, 0).start()

    each_group(before_pf, prefix_forward, after_pf)

    def after_pb(g, h):
        if h == 1:
            pre_sum_core(g)
        if (g, h) == (1, 0):
            pre_sum_z(0)

    def after_wb(g, h):
        if (g, h) == (0, 1):
            pre_sum_z(1)
        if (g, h) == (0, 0):
            win_sum_core(0)
        if (g, h) == (1, 1):
            win_sum_x(0)
            pre_sum_x(1)
        if (g, h) == (1, 0):
            win_sum_core(1)
            pre_sum_home(0)

    def after_dq(g, h):
        if (g, h) == (1, 1):
            win_sum_x(1)
        for i in of_half[h]:
            q_back(g, i, 1).start()
        if (g, h) == (0, 1):
            pre_sum_x(0)
        if (g, h) == (1, 0):
            pre_sum_home(1)
            sum_back(0)
            sum_back(1)

    def at_group(g, h, after):
        for k in range(GROUPS):
            @pl.when(g == k)
            def _():
                after(k, h)

    def pb_body(g, carry):
        for k in range(GROUPS):
            @pl.when(g == k)
            def _():
                q_wait(k, 1)
        for h in (0, 1):
            gradients(g, h, 0)
            at_group(g, h, after_pb)
        return carry

    def wb_body(g, carry):
        for work, after in ((window_backward, after_wb), (query_gradients, after_dq)):
            for h in (1, 0):
                work(g, h)
                at_group(g, h, after)
        return carry

    lax.fori_loop(0, GROUPS, pb_body, 0)
    lax.fori_loop(0, GROUPS, wb_body, 0)


    for g in range(GROUPS):
        for n in range(2):
            arrived(("back", g, n), out_buf.at[g, 0:3 * BLK, :])
            q_back(g, 3, n).wait()
            k_back(g, 3, n).wait()
            left(("q", g, n), q_in.at[g, 0:3 * BLK, :])
            left(("back", g, n), out_buf.at[g, 0:3 * BLK, :])
        arrived(("kback", g), size_of(6 * BLK))
        left(("kback", g), size_of(6 * BLK))
        left(("kv", g), size_of(6 * BLK))
        left(("z", g), size_of(12 * QUARTER))
        left(("zsum", g), z_buf.at[g])
        for step in range(1, 4):
            for u in range(2):
                @pl.when(x == (u + step) % 4)
                def _():
                    x_sum(g, u, step).wait_send()

            @pl.when((x < 2) & (z == step))
            def _():
                home(g, step).wait_send()

        for u in range(2):
            half_unit(g, u).wait_send()
        for i in range(4):
            core_sum(g, i).wait_send()

        for ahead in (1, 2):
            @pl.when(slab + ahead < 16)
            def _():
                window(g, ahead).wait_send()

            @pl.when(slab >= ahead)
            def _():
                w_sum(g, ahead).wait_send()

        @pl.when(core == 0)
        def _():
            core_own(g).wait_send()

            @pl.when(slab >= 1)
            def _():
                near_up(g).wait_send()

        @pl.when(core == 1)
        def _():
            @pl.when(slab >= 1)
            def _():
                near_down(g).wait_send()

            @pl.when(slab >= 2)
            def _():
                far_down(g).wait_send()

    @pl.when(source)
    def _():
        left(("ins", True), size_of(12 * BLK))

        @pl.when(jnp.logical_not(alone))
        def _():
            left(("ins", False), size_of(4 * BLK))

    @pl.when(spreads)
    def _():
        left(("xs",), size_of(12 * QUARTER))

    assert (len(sends), len(arrivals)) == (SENDS, ARRIVALS), (len(sends), len(arrivals))


def store_kernel(*refs):
    src, dst, held = refs[:4], refs[4:8], refs[8:12]
    into, out = refs[12:]
    parts = [(a, b * BLK // n, BLK // n, b) for a, n in enumerate((4, 4, 1, 1)) for b in range(n)]

    def load(a, at, count, b):
        return pltpu.make_async_copy(src[a].at[pl.ds(at, count)], held[a].at[pl.ds(at, count)], into.at[a, b])

    def save(a, at, count, b):
        return pltpu.make_async_copy(held[a].at[pl.ds(at, count)], dst[a].at[pl.ds(at, count)], out.at[a, b])

    for part in parts:
        load(*part).start()
    for part in parts:
        load(*part).wait()
        save(*part).start()
    for part in parts:
        save(*part).wait()


def on_device(queries, keys, values, grad_out, doc_lengths, share_prefix):
    anywhere = pl.BlockSpec(memory_space=pl.ANY)
    smem = pl.BlockSpec(memory_space=pltpu.SMEM)
    unit = (2, UNIT, HD)
    G = GROUPS
    results = pl.pallas_call(
        kernel,
        in_specs=[smem, smem] + [anywhere] * 4,
        out_specs=[anywhere] * 4,
        out_shape=[
            jax.ShapeDtypeStruct((BLK, QH * HD), BF),
            jax.ShapeDtypeStruct((BLK, QH * HD), BF),
            jax.ShapeDtypeStruct((BLK, KVH * HD), BF),
            jax.ShapeDtypeStruct((BLK, KVH * HD), BF),
        ],
        scratch_shapes=[
            pltpu.VMEM((G, UNIT, WIDE), BF),
            pltpu.VMEM((G, UNIT, WIDE), BF),
            pltpu.VMEM((G, 2, KEYS, HD), BF),
            pltpu.VMEM((G, 2, HD, KEYS), BF),
            pltpu.VMEM((2, SPAN, LANES), F32),
            pltpu.VMEM((G, 2, SPAN, LANES), BF),
            pltpu.VMEM((G, 2, PRE, LANES), BF),
            pltpu.VMEM((G, 2, LANES, HD), BF),
            pltpu.VMEM((2, HD, LANES), BF),
            pltpu.VMEM((2, G, 2, HD, LANES), F32),
            pltpu.VMEM((G, 2, HD, LANES), BF),
            pltpu.VMEM((G, 2, HD, LANES), BF),
            pltpu.VMEM((2, 8, LANES), jnp.int32),
            pltpu.VMEM((G, 2, 8, LANES), F32),
            pltpu.VMEM((KEYS, HD), F32),
            pltpu.VMEM((KEYS, HD), F32),
            pltpu.VMEM((G, UNIT, WIDE), BF),
            pltpu.VMEM((G, UNIT, WIDE), BF),
            pltpu.VMEM((G, 2, KEYS, HD), BF),
            pltpu.VMEM((G, 4) + unit, BF),
            pltpu.VMEM((G, 2) + unit, BF),
            pltpu.VMEM((G, 3, 2, 2, QUARTER, HD), BF),
            pltpu.VMEM((G, 2, 2, QUARTER, HD), BF),
            pltpu.VMEM((G, 3, 2, QUARTER, HD), BF),
            pltpu.VMEM((G, 2, QUARTER, HD), BF),
            pltpu.VMEM((G,) + unit, BF),
            pltpu.VMEM((G, 2) + unit, BF),
            pltpu.VMEM((G, 2) + unit, BF),
            pltpu.VMEM((G,) + unit, F32),
            pltpu.VMEM((G,) + unit, BF),
            pltpu.SemaphoreType.DMA((SENDS,)),
            pltpu.SemaphoreType.DMA((ARRIVALS,)),
            pltpu.SemaphoreType.DMA((22,)),
        ],
        compiler_params=pltpu.CompilerParams(
            collective_id=0, has_side_effects=True, vmem_limit_bytes=60 * 1024 * 1024
        ),
        name="packed_attention",
    )(doc_lengths, share_prefix, queries, grad_out, keys, values)
    return tuple(pl.pallas_call(
        store_kernel,
        in_specs=[anywhere] * 4,
        out_specs=[anywhere] * 4,
        out_shape=[jax.ShapeDtypeStruct(a.shape, a.dtype) for a in results],
        scratch_shapes=[pltpu.VMEM(a.shape, a.dtype) for a in results] + [pltpu.SemaphoreType.DMA((4, 4))] * 2,
        name="store_results",
    )(*results))


def solution(mesh):
    rows = P(("ctx", "heads"), None)
    return jax.shard_map(
        on_device, mesh=mesh, in_specs=(rows, rows, rows, rows, P(), P()),
        out_specs=(rows, rows, rows, rows), check_vma=False,
    )
```

```python
import jax
import jax.numpy as jnp
from jax import lax
from jax.experimental import pallas as pl
from jax.experimental.pallas import tpu as pltpu
from jax.sharding import PartitionSpec as P

QH = 64
KVH = 8
HD = 128
PER = QH // KVH
DOCS = 16
MESH = pl.DeviceIdType.MESH
BF = jnp.bfloat16
F32 = jnp.float32

UNIT = 256
BLK = 64
BACK = 4
PRE = 1024
KEYS = PRE + (BACK + 1) * UNIT
GROUPS = 2
WIDE = PER * HD

ROWS = 128
LANES = PER * ROWS
KC = 512
SPAN = BACK * UNIT + ROWS
SCALE = HD ** (-0.5)
LOG2E = 1.4426950408889634
QUARTER = UNIT // 4
SENDS, ARRIVALS = 49, 59
NT = (((1,), (1,)), ((), ()))


def kernel(
    lens, share, q_ref, do_ref, k_ref, v_ref, o_ref, odq_ref, dk_ref, dv_ref,
    q_in, do_in, kv, kt, s_scr, p_win, p_pre, q_scr, dot_scr, acc, out_t, do_t, lim, stat, gk, gv,
    out_buf, dq_buf, g_buf, core_buf, z_send, z_buf, x_send, x_buf, last_send, last_buf, w_send, w_buf,
    sum_buf, k_buf, send, recv, local,
):
    ctx = lax.axis_index("ctx")
    y = lax.axis_index("heads")
    core = ctx % 2
    slab = ctx // 2
    z = slab // 4
    x = slab % 4
    mine = pl.multiple_of(y * BLK, BLK)
    own = PRE + BACK * UNIT
    slot = [PRE + i * UNIT for i in range(BACK + 1)]
    first = ctx * UNIT
    base = first - BACK * UNIT - PRE

    def device(to_slab, to_core, to_y):
        return {"ctx": to_slab * 2 + to_core, "heads": to_y}

    sibling = device(slab, 1 - core, y)
    peers = [y + 1 - 2 * (y % 2), 3 - y, (y + 2) % 4]
    halves = [y // 2, 1 - y // 2]
    of_half = ((0, 3), (1, 2))

    @pl.when(slab < 2)
    def _():
        for g in range(GROUPS):
            kv[g, :, PRE:own, :] = jnp.zeros((2, BACK * UNIT, HD), BF)

    barrier = pltpu.get_barrier_semaphore()

    def greet(to):
        pl.semaphore_signal(barrier, inc=1, device_id=to, device_id_type=MESH)

    for step in range(1, 4):
        greet(device(z * 4 + (x + step) % 4, core, y))
        greet(device((slab + 4 * step) % 16, core, y))
        greet(device(slab, core, (y + step) % 4))
    for step in (1, 2, 14, 15):
        greet(device((slab + step) % 16, core, y))
    greet(sibling)
    source = slab < 2
    spreads = x < 2
    alone = (z == 0) & (y == 0)

    @pl.when(source)
    def _():
        for step in range(4):
            @pl.when(jnp.logical_not(alone) | (step > 0))
            def _():
                greet(device(y * 4 + x, core, (y + step) % 4))

    @pl.when(spreads & jnp.logical_not(alone))
    def _():
        greet(device(x, core, z))

    for h in range(2):
        pos = first + halves[h] * ROWS + lax.broadcasted_iota(jnp.int32, (1, LANES), 1) % ROWS
        start_i = jnp.zeros((1, LANES), jnp.int32)
        share_i = jnp.zeros((1, LANES), jnp.int32)
        begin = lens[0]
        for d in range(1, DOCS):
            inside = pos >= begin
            start_i = jnp.where(inside, begin, start_i)
            share_i = jnp.where(inside, share[d], share_i)
            begin = begin + lens[d]
        w_at = PRE + halves[h] * ROWS
        lim[h, 0:1, :] = jnp.where(share_i == 1, lens[0], 0)
        lim[h, 1:2, :] = start_i - base - w_at
        lim[h, 2:3, :] = pos - base - w_at

    one = jnp.where(alone, 1, 0)
    pl.semaphore_wait(barrier, 14 + jnp.where(source, 4 - one, 0) + jnp.where(spreads, 1 - one, 0))

    sends, arrivals = {}, {}

    def remote(name, src, dst, to, sent=None):
        at = arrivals.setdefault(name, len(arrivals))
        out = sends.setdefault(name if sent is None else sent, len(sends))
        return pltpu.make_async_remote_copy(
            src_ref=src, dst_ref=dst, send_sem=send.at[out], recv_sem=recv.at[at],
            device_id=to, device_id_type=MESH,
        )

    def arrived(name, size):
        pltpu.make_async_copy(size, size, recv.at[arrivals[name]]).wait()

    def left(name, size):
        pltpu.make_async_copy(size, size, send.at[sends[name]]).wait()

    def size_of(count):
        return kv.at[0, 0, 0:count, :]


    def columns(ref, to, g):
        return ref.at[:, pl.ds(pl.multiple_of((to * GROUPS + g) * HD, HD), HD)]

    def kv_head(g, i, n):
        ref = (k_ref, v_ref)[n]
        to = (peers + [y])[i]
        src = ref.at[:, pl.ds(pl.multiple_of((to * GROUPS + g) * HD, HD), HD)]
        dst = kv.at[g, n, pl.ds(own + mine, BLK), :]
        if i == 3:
            return pltpu.make_async_copy(src, dst, local.at[g * 2 + n])
        return remote(("kv", g), src, dst, device(slab, core, to))

    def q_head(g, i, n):
        ref, into = ((q_ref, q_in), (do_ref, do_in))[n]
        to = (peers + [y])[i]
        src = ref.at[:, pl.ds(pl.multiple_of((to * GROUPS + g) * WIDE, WIDE), WIDE)]
        dst = into.at[g, pl.ds(mine, BLK), :]
        if i == 3:
            return pltpu.make_async_copy(src, dst, local.at[4 + g * 2 + n])
        return remote(("q", g, n), src, dst, device(slab, core, to))

    def rows(g, at, count):
        return kv.at[g, :, pl.ds(at, count), :]

    def move(name, g, src, dst, count, to):
        return remote((name, g), rows(g, src, count), rows(g, dst, count), to)

    def unit_at(u):
        return pl.multiple_of((core + 2 * u) * UNIT, UNIT)

    def spread_in(g, step, n):
        src = columns((k_ref, v_ref)[n], (y + step) % 4, g)
        dst = kv.at[g, n, pl.ds(pl.multiple_of(unit_at(x) + mine, BLK), BLK), :]
        return remote(
            ("in",), src, dst, device(y * 4 + x, core, (y + step) % 4), sent=("ins", step > 0)
        )

    def spread_own(g, n):
        src = columns((k_ref, v_ref)[n], y, g)
        return pltpu.make_async_copy(
            src, kv.at[g, n, pl.ds(pl.multiple_of(unit_at(x) + mine, BLK), BLK), :], local.at[18 + g * 2 + n]
        )

    def quarter(u):
        return kv.at[:, :, pl.ds(pl.multiple_of(unit_at(u) + z * QUARTER, QUARTER), QUARTER), :]

    def along_x(u, step):
        return remote(
            ("x", u, step), quarter(u), quarter(u), device(z * 4 + (u + step) % 4, core, y), sent=("xs",)
        )

    def along_z(g, u, step):
        at = pl.multiple_of(unit_at(u) + z * QUARTER, QUARTER)
        return move("z", g, at, at, QUARTER, device((slab + 4 * step) % 16, core, y))

    def half_unit(g, u):
        return move(("half", u), g, unit_at(u), unit_at(u), UNIT, sibling)

    def window(g, ahead):
        return move(
            ("window", ahead), g, own, slot[2] if ahead == 1 else slot[0], UNIT,
            device((slab + ahead) % 16, core, y),
        )

    def core_own(g):
        return move(("core", 3), g, own, slot[3], UNIT, sibling)

    def near_up(g):
        return move(("core", 1), g, slot[2], slot[1], UNIT, sibling)

    def near_down(g):
        return move(("core", 3), g, slot[2], slot[3], UNIT, sibling)

    def far_down(g):
        return move(("core", 1), g, slot[0], slot[1], UNIT, sibling)

    def q_start(g, n):
        for i in (0, 3, 1, 2):
            q_head(g, i, n).start()

    def q_wait(g, n):
        arrived(("q", g, n), q_in.at[g, 0:3 * BLK, :])
        q_head(g, 3, n).wait()

    def kv_start(g):
        for i in range(4):
            for n in range(2):
                kv_head(g, i, n).start()

    def kv_units(g):
        arrived(("kv", g), size_of(6 * BLK))
        for n in range(2):
            kv_head(g, 3, n).wait()
        for ahead in (1, 2):
            @pl.when(slab + ahead < 16)
            def _():
                window(g, ahead).start()

        @pl.when(core == 0)
        def _():
            core_own(g).start()

    def pre_in():
        @pl.when(source)
        def _():
            for g in range(GROUPS):
                for n in range(2):
                    @pl.when(jnp.logical_not(alone))
                    def _():
                        spread_in(g, 0, n).start()

                    @pl.when(alone)
                    def _():
                        spread_own(g, n).start()

                    for step in range(1, 4):
                        spread_in(g, step, n).start()

    def pre_x():
        for u in range(2):
            @pl.when(x == u)
            def _():
                @pl.when(jnp.logical_not(alone))
                def _():
                    arrived(("in",), size_of(4 * BLK))

                @pl.when(alone)
                def _():
                    for g in range(GROUPS):
                        for n in range(2):
                            spread_own(g, n).wait()

                for step in (2, 1, 3):
                    along_x(u, step).start()

    def pre_z():
        for u in range(2):
            for step in range(1, 4):
                @pl.when(x == (u + step) % 4)
                def _():
                    along_x(u, step).wait_recv()
        for g in range(GROUPS):
            for step in (2, 1, 3):
                for u in range(2):
                    along_z(g, u, step).start()

    def pre_core(g):
        arrived(("z", g), size_of(12 * QUARTER))
        for u in range(2):
            half_unit(g, u).start()

    def pre_done(g):
        for u in range(2):
            half_unit(g, u).wait_recv()

    def win_core(g):
        @pl.when(slab >= 1)
        def _():
            window(g, 1).wait_recv()

            @pl.when(core == 0)
            def _():
                near_up(g).start()

            @pl.when(core == 1)
            def _():
                near_down(g).start()

        @pl.when(slab >= 2)
        def _():
            window(g, 2).wait_recv()

            @pl.when(core == 1)
            def _():
                far_down(g).start()

    def win_done(g):
        @pl.when(core == 1)
        def _():
            core_own(g).wait_recv()

            @pl.when(slab >= 1)
            def _():
                near_up(g).wait_recv()

        @pl.when(core == 0)
        def _():
            @pl.when(slab >= 1)
            def _():
                near_down(g).wait_recv()

            @pl.when(slab >= 2)
            def _():
                far_down(g).wait_recv()


    def q_back(g, i, n):
        buf, ref = ((out_buf, o_ref), (dq_buf, odq_ref))[n]
        to = (peers + [y])[i]
        src = buf.at[g, pl.ds(pl.multiple_of(to * BLK, BLK), BLK), :]
        dst = ref.at[:, pl.ds(pl.multiple_of((y * GROUPS + g) * WIDE, WIDE), WIDE)]
        if i == 3:
            return pltpu.make_async_copy(src, dst, local.at[10 + g * 2 + n])
        return remote(("back", g, n), src, dst, device(slab, core, to))

    def core_sum(g, i):
        at = unit_at(i) + (1 - 2 * core) * UNIT if i < 2 else slot[1 + 2 * (i - 2)]
        if i < 2:
            at = pl.multiple_of(at, UNIT)
        return remote(("csum", g, i), g_buf.at[g, :, pl.ds(at, UNIT), :], core_buf.at[g, i], sibling)

    def z_sum(g, step):
        at = pl.multiple_of(((z + step) % 4) * QUARTER, QUARTER)
        return remote(
            ("zsum", g), z_send.at[g, :, :, pl.ds(at, QUARTER), :], z_buf.at[g, step - 1],
            device((slab + 4 * step) % 16, core, y),
        )

    def x_sum(g, u, step):
        return remote(
            ("xsum", g, step), x_send.at[g, u], x_buf.at[g, step - 1], device(z * 4 + u, core, y),
            sent=("xsums", g, u),
        )

    def home(g, step):
        at = pl.multiple_of(z * QUARTER, QUARTER)
        return remote(
            ("home", g, step), last_send.at[g], last_buf.at[g, :, pl.ds(at, QUARTER), :], device(x, core, y),
            sent=("homes", g),
        )

    def w_sum(g, back):
        return remote(
            ("wsum", g, back), w_send.at[g, back - 1], w_buf.at[g, back - 1],
            device((slab + 16 - back) % 16, core, y),
        )

    def k_back(g, i, n):
        ref = (dk_ref, dv_ref)[n]
        to = (peers + [y])[i]
        src = k_buf.at[g, n, pl.ds(pl.multiple_of(to * BLK, BLK), BLK), :]
        dst = ref.at[:, pl.ds(pl.multiple_of((y * GROUPS + g) * HD, HD), HD)]
        if i == 3:
            return pltpu.make_async_copy(src, dst, local.at[14 + g * 2 + n])
        return remote(("kback", g), src, dst, device(slab, core, to))

    def pre_sum_core(g):
        for i in range(2):
            core_sum(g, i).start()

    def pre_sum_z(g):
        for i in range(2):
            core_sum(g, i).wait_recv()
            z_send[g, i] = (
                g_buf[g, :, pl.ds(unit_at(i), UNIT), :].astype(F32) + core_buf[g, i].astype(F32)
            ).astype(BF)
        for step in range(1, 4):
            z_sum(g, step).start()

    def pre_sum_x(g):
        arrived(("zsum", g), z_buf.at[g])
        total = z_send[g, :, :, pl.ds(pl.multiple_of(z * QUARTER, QUARTER), QUARTER), :].astype(F32)
        for i in range(3):
            total += z_buf[g, i].astype(F32)
        x_send[g] = total.astype(BF)
        for u in range(2):
            for step in range(1, 4):
                @pl.when(x == (u + step) % 4)
                def _():
                    x_sum(g, u, step).start()

    def pre_sum_home(g):
        for u in range(2):
            @pl.when(x == u)
            def _():
                total = x_send[g, u].astype(F32)
                for step in range(1, 4):
                    x_sum(g, u, step).wait_recv()
                    total += x_buf[g, step - 1].astype(F32)
                last_send[g] = total.astype(BF)
                for step in range(1, 4):
                    @pl.when(z == step)
                    def _():
                        home(g, step).start()

    def win_sum_core(g):
        for i in (2, 3):
            core_sum(g, i).start()

    def win_sum_x(g):
        core_sum(g, 2).wait_recv()
        core_sum(g, 3).wait_recv()
        a = core_buf[g, 2].astype(F32)
        b = core_buf[g, 3].astype(F32)
        lower = core == 0
        far = g_buf[g, :, slot[0]:slot[0] + UNIT, :].astype(F32)
        near = g_buf[g, :, slot[2]:slot[2] + UNIT, :].astype(F32)
        here = g_buf[g, :, slot[4]:slot[4] + UNIT, :].astype(F32)
        w_send[g, 1] = (far + jnp.where(lower, 0.0, a)).astype(BF)
        w_send[g, 0] = (near + jnp.where(lower, a, b)).astype(BF)
        for back in (2, 1):
            @pl.when(slab >= back)
            def _():
                w_sum(g, back).start()
        sum_buf[g] = here + jnp.where(lower, b, 0.0)

    def sum_back(g):
        @pl.when(slab < 2)
        def _():
            for step in range(1, 4):
                home_at = step * QUARTER
                remote(
                    ("home", g, step), last_send.at[g], last_buf.at[g, :, pl.ds(home_at, QUARTER), :], sibling,
                    sent=("homes", g),
                ).wait_recv()
            last_buf[g, :, 0:QUARTER, :] = last_send[g]
            sum_buf[g] += last_buf[g].astype(F32)

        for back in (1, 2):
            @pl.when(slab + back < 16)
            def _():
                w_sum(g, back).wait_recv()
                sum_buf[g] += w_buf[g, back - 1].astype(F32)

        k_buf[g] = sum_buf[g].astype(BF)
        for i in (2, 1, 0, 3):
            for n in range(2):
                k_back(g, i, n).start()


    def blocks_of(part, h):
        if part == 0:
            return [(at, at, KC) for at in range(0, PRE, KC)]
        w_at = PRE + halves[h] * ROWS
        blocks = [(pl.multiple_of(w_at + at, ROWS), at, KC) for at in range(0, BACK * UNIT, KC)]
        return blocks + [(pl.multiple_of(w_at + BACK * UNIT, ROWS), BACK * UNIT, ROWS)]

    def place(h):
        return pl.ds(pl.multiple_of(halves[h] * ROWS, ROWS), ROWS)

    def scores(g, h, part, state):
        state["top"] = jnp.full((8, LANES), -1e30, F32)

        def step(src, at, count):
            s = lax.dot_general(
                kv[g, 0, pl.ds(src, count), :], q_scr[g, h], NT, preferred_element_type=F32
            )
            j = lax.broadcasted_iota(jnp.int32, (count, LANES), 0)
            if part == 0:
                ok = j < lim[h, 0:1, :] - at
            else:
                ok = j >= lim[h, 1:2, :] - at
                if count == ROWS:
                    ok &= j <= lim[h, 2:3, :] - at
            s = jnp.where(ok, s, -1e30)
            s_scr[h, at:at + count, :] = s
            state["top"] = jnp.maximum(state["top"], jnp.max(s.reshape(count // 8, 8, LANES), axis=0))

        return [lambda b=b: step(*b) for b in blocks_of(part, h)]

    def weighted(g, h, part, state):
        p_scr = (p_pre, p_win)[part]

        def step(src, at, count):
            if at == 0:
                state["mc"] = jnp.max(state["top"], axis=0, keepdims=True) * (SCALE * LOG2E)
                state["sum"] = jnp.zeros((8, LANES), F32)
            p = jnp.exp2(s_scr[h, at:at + count, :] * (SCALE * LOG2E) - state["mc"])
            state["sum"] += jnp.sum(p.reshape(count // 8, 8, LANES), axis=0)
            pb = p.astype(BF)
            p_scr[g, h, at:at + count, :] = pb
            o = jnp.dot(kt[g, 1, :, pl.ds(src, count)], pb, preferred_element_type=F32)
            spot = acc.at[part, g, h]
            if at == 0:
                spot[...] = o
            else:
                spot[...] += o

        return [lambda b=b: step(*b) for b in blocks_of(part, h)]

    def turn(g, low, count):
        for n in range(2):
            kt[g, n, :, low:low + count] = kv[g, n, low:low + count, :].astype(F32).T.astype(BF)

    def both(g, part):
        state = [{}, {}]
        for step in scores(g, 0, part, state[0]):
            step()
        late = scores(g, 1, part, state[1])
        for step in weighted(g, 0, part, state[0]):
            late.pop(0)()
            step()
        for step in weighted(g, 1, part, state[1]):
            step()
        return state

    def window_forward(g):
        for h in range(2):
            for i in range(PER):
                q_scr[g, h, i * ROWS:(i + 1) * ROWS, :] = q_in[g, place(h), i * HD:(i + 1) * HD]
        turn(g, PRE, KEYS - PRE)
        state = both(g, 1)
        for h in range(2):
            stat[g, h, 0:1, :] = state[h]["mc"]
            stat[g, h, 1:2, :] = jnp.sum(state[h]["sum"], axis=0, keepdims=True)

    def prefix_forward(g):
        turn(g, 0, PRE)
        state = both(g, 0)
        for h in range(2):
            mw = stat[g, h, 0:1, :]
            lw = stat[g, h, 1:2, :]
            mp = state[h]["mc"]
            lp = jnp.sum(state[h]["sum"], axis=0, keepdims=True)
            m = jnp.maximum(mw, mp)
            aw = jnp.exp2(mw - m)
            ap = jnp.exp2(mp - m)
            inv = 1.0 / (aw * lw + ap * lp)
            fp = ap * inv
            fw = aw * inv
            stat[g, h, 0:1, :] = fp
            stat[g, h, 1:2, :] = fw
            o = acc[0, g, h] * fp + acc[1, g, h] * fw
            out_t[g, h] = o.astype(BF)
            out = o.T.astype(BF)
            for i in range(PER):
                out_buf[g, place(h), i * HD:(i + 1) * HD] = out[i * ROWS:(i + 1) * ROWS, :]

    def gradients(g, h, part):
        p_scr = (p_pre, p_win)[part]
        if part == 0:
            for i in range(PER):
                do_t[g, h, :, i * ROWS:(i + 1) * ROWS] = (
                    do_in[g, place(h), i * HD:(i + 1) * HD].astype(F32).T.astype(BF)
                )
        factor = stat[g, h, part:part + 1, :]
        scaled = (do_t[g, h].astype(F32) * factor).astype(BF)
        dot_scr[h] = scaled
        delta = jnp.sum(scaled.astype(F32) * out_t[g, h].astype(F32), axis=0, keepdims=True)
        first_half = h == (0 if part == 0 else 1)
        for src, at, count in blocks_of(part, h):
            dp = jnp.dot(kv[g, 1, pl.ds(src, count), :], dot_scr[h], preferred_element_type=F32)
            pb = p_scr[g, h, at:at + count, :]
            ds = (pb.astype(F32) * (dp - delta)).astype(BF)
            tv = lax.dot_general(pb, dot_scr[h], NT, preferred_element_type=F32)
            tk = jnp.dot(ds, q_scr[g, h], preferred_element_type=F32)
            if first_half:
                gv[pl.ds(src, count), :] = tv
                gk[pl.ds(src, count), :] = tk
            else:
                g_buf[g, 1, pl.ds(src, count), :] = (gv[pl.ds(src, count), :] + tv).astype(BF)
                g_buf[g, 0, pl.ds(src, count), :] = ((gk[pl.ds(src, count), :] + tk) * SCALE).astype(BF)
            p_scr[g, h, at:at + count, :] = ds

    def window_backward(g, h):
        apart = [pl.ds(pl.multiple_of(PRE + halves[1 - i] * SPAN, ROWS), ROWS) for i in range(2)]
        if h == 1:
            zero = jnp.zeros((ROWS, HD), F32)
            gk[apart[1], :] = zero
            gv[apart[1], :] = zero
        gradients(g, h, 1)
        if h == 0:
            g_buf[g, 1, apart[0], :] = gv[apart[0], :].astype(BF)
            g_buf[g, 0, apart[0], :] = (gk[apart[0], :] * SCALE).astype(BF)

    def query_gradients(g, h):
        w_at = pl.multiple_of(PRE + halves[h] * ROWS, ROWS)
        o = jnp.dot(kt[g, 0, :, 0:PRE], p_pre[g, h], preferred_element_type=F32)
        o += jnp.dot(kt[g, 0, :, pl.ds(w_at, SPAN)], p_win[g, h], preferred_element_type=F32)
        dq = (o * SCALE).T.astype(BF)
        for i in range(PER):
            dq_buf[g, place(h), i * HD:(i + 1) * HD] = dq[i * ROWS:(i + 1) * ROWS, :]


    def each_group(before, work, after):
        def body(g, carry):
            for k in range(GROUPS):
                @pl.when(g == k)
                def _():
                    before(k)
            work(g)
            for k in range(GROUPS):
                @pl.when(g == k)
                def _():
                    after(k)
            return carry

        lax.fori_loop(0, GROUPS, body, 0)

    pre_in()
    kv_start(0)
    kv_start(1)
    q_start(0, 0)
    pre_x()
    kv_units(0)
    q_start(1, 0)
    pre_z()
    kv_units(1)
    q_start(0, 1)
    q_start(1, 1)
    win_core(0)

    def before_wf(g):
        if g == 1:
            win_core(1)
        q_wait(g, 0)
        win_done(g)

    def after_wf(g):
        if g == 0:
            pre_core(0)

    each_group(before_wf, window_forward, after_wf)

    def before_pf(g):
        if g == 0:
            pre_core(1)
        pre_done(g)

    def after_pf(g):
        for i in (1, 2, 0, 3):
            q_back(g, i, 0).start()

    each_group(before_pf, prefix_forward, after_pf)

    def after_pb(g, h):
        if h == 1:
            pre_sum_core(g)
        if (g, h) == (1, 0):
            pre_sum_z(0)

    def after_wb(g, h):
        if (g, h) == (0, 1):
            pre_sum_z(1)
        if (g, h) == (0, 0):
            win_sum_core(0)
        if (g, h) == (1, 1):
            pre_sum_x(1)
        if (g, h) == (1, 0):
            win_sum_core(1)
            pre_sum_home(0)

    def after_dq(g, h):
        if (g, h) == (1, 1):
            win_sum_x(1)
        for i in of_half[h]:
            q_back(g, i, 1).start()
        if (g, h) == (0, 1):
            pre_sum_x(0)
        if (g, h) == (0, 0):
            win_sum_x(0)
        if (g, h) == (1, 0):
            pre_sum_home(1)
            sum_back(0)
            sum_back(1)

    def at_group(g, h, after):
        for k in range(GROUPS):
            @pl.when(g == k)
            def _():
                after(k, h)

    def pb_body(g, carry):
        for k in range(GROUPS):
            @pl.when(g == k)
            def _():
                q_wait(k, 1)
        for h in (0, 1):
            gradients(g, h, 0)
            at_group(g, h, after_pb)
        return carry

    def wb_body(g, carry):
        for work, after in ((window_backward, after_wb), (query_gradients, after_dq)):
            for h in (1, 0):
                work(g, h)
                at_group(g, h, after)
        return carry

    lax.fori_loop(0, GROUPS, pb_body, 0)
    lax.fori_loop(0, GROUPS, wb_body, 0)


    for g in range(GROUPS):
        for n in range(2):
            arrived(("back", g, n), out_buf.at[g, 0:3 * BLK, :])
            q_back(g, 3, n).wait()
            k_back(g, 3, n).wait()
            left(("q", g, n), q_in.at[g, 0:3 * BLK, :])
            left(("back", g, n), out_buf.at[g, 0:3 * BLK, :])
        arrived(("kback", g), size_of(6 * BLK))
        left(("kback", g), size_of(6 * BLK))
        left(("kv", g), size_of(6 * BLK))
        left(("z", g), size_of(12 * QUARTER))
        left(("zsum", g), z_buf.at[g])
        for step in range(1, 4):
            for u in range(2):
                @pl.when(x == (u + step) % 4)
                def _():
                    x_sum(g, u, step).wait_send()

            @pl.when((x < 2) & (z == step))
            def _():
                home(g, step).wait_send()

        for u in range(2):
            half_unit(g, u).wait_send()
        for i in range(4):
            core_sum(g, i).wait_send()

        for ahead in (1, 2):
            @pl.when(slab + ahead < 16)
            def _():
                window(g, ahead).wait_send()

            @pl.when(slab >= ahead)
            def _():
                w_sum(g, ahead).wait_send()

        @pl.when(core == 0)
        def _():
            core_own(g).wait_send()

            @pl.when(slab >= 1)
            def _():
                near_up(g).wait_send()

        @pl.when(core == 1)
        def _():
            @pl.when(slab >= 1)
            def _():
                near_down(g).wait_send()

            @pl.when(slab >= 2)
            def _():
                far_down(g).wait_send()

    @pl.when(source)
    def _():
        left(("ins", True), size_of(12 * BLK))

        @pl.when(jnp.logical_not(alone))
        def _():
            left(("ins", False), size_of(4 * BLK))

    @pl.when(spreads)
    def _():
        left(("xs",), size_of(12 * QUARTER))

    assert (len(sends), len(arrivals)) == (SENDS, ARRIVALS), (len(sends), len(arrivals))


def store_kernel(*refs):
    src, dst, held = refs[:4], refs[4:8], refs[8:12]
    into, out = refs[12:]
    parts = [(a, b * BLK // n, BLK // n, b) for a, n in enumerate((4, 4, 1, 1)) for b in range(n)]

    def load(a, at, count, b):
        return pltpu.make_async_copy(src[a].at[pl.ds(at, count)], held[a].at[pl.ds(at, count)], into.at[a, b])

    def save(a, at, count, b):
        return pltpu.make_async_copy(held[a].at[pl.ds(at, count)], dst[a].at[pl.ds(at, count)], out.at[a, b])

    for part in parts:
        load(*part).start()
    for part in parts:
        load(*part).wait()
        save(*part).start()
    for part in parts:
        save(*part).wait()


def on_device(queries, keys, values, grad_out, doc_lengths, share_prefix):
    anywhere = pl.BlockSpec(memory_space=pl.ANY)
    smem = pl.BlockSpec(memory_space=pltpu.SMEM)
    unit = (2, UNIT, HD)
    G = GROUPS
    results = pl.pallas_call(
        kernel,
        in_specs=[smem, smem] + [anywhere] * 4,
        out_specs=[anywhere] * 4,
        out_shape=[
            jax.ShapeDtypeStruct((BLK, QH * HD), BF),
            jax.ShapeDtypeStruct((BLK, QH * HD), BF),
            jax.ShapeDtypeStruct((BLK, KVH * HD), BF),
            jax.ShapeDtypeStruct((BLK, KVH * HD), BF),
        ],
        scratch_shapes=[
            pltpu.VMEM((G, UNIT, WIDE), BF),
            pltpu.VMEM((G, UNIT, WIDE), BF),
            pltpu.VMEM((G, 2, KEYS, HD), BF),
            pltpu.VMEM((G, 2, HD, KEYS), BF),
            pltpu.VMEM((2, SPAN, LANES), F32),
            pltpu.VMEM((G, 2, SPAN, LANES), BF),
            pltpu.VMEM((G, 2, PRE, LANES), BF),
            pltpu.VMEM((G, 2, LANES, HD), BF),
            pltpu.VMEM((2, HD, LANES), BF),
            pltpu.VMEM((2, G, 2, HD, LANES), F32),
            pltpu.VMEM((G, 2, HD, LANES), BF),
            pltpu.VMEM((G, 2, HD, LANES), BF),
            pltpu.VMEM((2, 8, LANES), jnp.int32),
            pltpu.VMEM((G, 2, 8, LANES), F32),
            pltpu.VMEM((KEYS, HD), F32),
            pltpu.VMEM((KEYS, HD), F32),
            pltpu.VMEM((G, UNIT, WIDE), BF),
            pltpu.VMEM((G, UNIT, WIDE), BF),
            pltpu.VMEM((G, 2, KEYS, HD), BF),
            pltpu.VMEM((G, 4) + unit, BF),
            pltpu.VMEM((G, 2) + unit, BF),
            pltpu.VMEM((G, 3, 2, 2, QUARTER, HD), BF),
            pltpu.VMEM((G, 2, 2, QUARTER, HD), BF),
            pltpu.VMEM((G, 3, 2, QUARTER, HD), BF),
            pltpu.VMEM((G, 2, QUARTER, HD), BF),
            pltpu.VMEM((G,) + unit, BF),
            pltpu.VMEM((G, 2) + unit, BF),
            pltpu.VMEM((G, 2) + unit, BF),
            pltpu.VMEM((G,) + unit, F32),
            pltpu.VMEM((G,) + unit, BF),
            pltpu.SemaphoreType.DMA((SENDS,)),
            pltpu.SemaphoreType.DMA((ARRIVALS,)),
            pltpu.SemaphoreType.DMA((22,)),
        ],
        compiler_params=pltpu.CompilerParams(
            collective_id=0, has_side_effects=True, vmem_limit_bytes=60 * 1024 * 1024
        ),
        name="packed_attention",
    )(doc_lengths, share_prefix, queries, grad_out, keys, values)
    return tuple(pl.pallas_call(
        store_kernel,
        in_specs=[anywhere] * 4,
        out_specs=[anywhere] * 4,
        out_shape=[jax.ShapeDtypeStruct(a.shape, a.dtype) for a in results],
        scratch_shapes=[pltpu.VMEM(a.shape, a.dtype) for a in results] + [pltpu.SemaphoreType.DMA((4, 4))] * 2,
        name="store_results",
    )(*results))


def solution(mesh):
    rows = P(("ctx", "heads"), None)
    return jax.shard_map(
        on_device, mesh=mesh, in_specs=(rows, rows, rows, rows, P(), P()),
        out_specs=(rows, rows, rows, rows), check_vma=False,
    )
```

```python
import jax
import jax.numpy as jnp
from jax import lax
from jax.experimental import pallas as pl
from jax.experimental.pallas import tpu as pltpu
from jax.sharding import PartitionSpec as P

QH = 64
KVH = 8
HD = 128
PER = QH // KVH
DOCS = 16
MESH = pl.DeviceIdType.MESH
BF = jnp.bfloat16
F32 = jnp.float32

UNIT = 256
BLK = 64
BACK = 4
PRE = 1024
KEYS = PRE + (BACK + 1) * UNIT
GROUPS = 2
WIDE = PER * HD

ROWS = 128
LANES = PER * ROWS
KC = 512
SPAN = BACK * UNIT + ROWS
SCALE = HD ** (-0.5)
LOG2E = 1.4426950408889634
QUARTER = UNIT // 4
SENDS, ARRIVALS = 49, 59
NT = (((1,), (1,)), ((), ()))


def kernel(
    lens, share, q_ref, do_ref, k_ref, v_ref, o_ref, odq_ref, dk_ref, dv_ref,
    q_in, do_in, kv, kt, s_scr, p_win, p_pre, q_scr, dot_scr, acc, out_t, do_t, lim, stat, gk, gv,
    out_buf, dq_buf, g_buf, core_buf, z_send, z_buf, x_send, x_buf, last_send, last_buf, w_send, w_buf,
    sum_buf, k_buf, send, recv, local,
):
    ctx = lax.axis_index("ctx")
    y = lax.axis_index("heads")
    core = ctx % 2
    slab = ctx // 2
    z = slab // 4
    x = slab % 4
    mine = pl.multiple_of(y * BLK, BLK)
    own = PRE + BACK * UNIT
    slot = [PRE + i * UNIT for i in range(BACK + 1)]
    first = ctx * UNIT
    base = first - BACK * UNIT - PRE

    def device(to_slab, to_core, to_y):
        return {"ctx": to_slab * 2 + to_core, "heads": to_y}

    sibling = device(slab, 1 - core, y)
    peers = [y + 1 - 2 * (y % 2), 3 - y, (y + 2) % 4]
    halves = [y // 2, 1 - y // 2]
    of_half = ((0, 3), (1, 2))

    @pl.when(slab < 2)
    def _():
        for g in range(GROUPS):
            kv[g, :, PRE:own, :] = jnp.zeros((2, BACK * UNIT, HD), BF)

    barrier = pltpu.get_barrier_semaphore()

    def greet(to):
        pl.semaphore_signal(barrier, inc=1, device_id=to, device_id_type=MESH)

    for step in range(1, 4):
        greet(device(z * 4 + (x + step) % 4, core, y))
        greet(device((slab + 4 * step) % 16, core, y))
        greet(device(slab, core, (y + step) % 4))
    for step in (1, 2, 14, 15):
        greet(device((slab + step) % 16, core, y))
    greet(sibling)
    source = slab < 2
    spreads = x < 2
    alone = (z == 0) & (y == 0)

    @pl.when(source)
    def _():
        for step in range(4):
            @pl.when(jnp.logical_not(alone) | (step > 0))
            def _():
                greet(device(y * 4 + x, core, (y + step) % 4))

    @pl.when(spreads & jnp.logical_not(alone))
    def _():
        greet(device(x, core, z))

    for h in range(2):
        pos = first + halves[h] * ROWS + lax.broadcasted_iota(jnp.int32, (1, LANES), 1) % ROWS
        start_i = jnp.zeros((1, LANES), jnp.int32)
        share_i = jnp.zeros((1, LANES), jnp.int32)
        begin = lens[0]
        for d in range(1, DOCS):
            inside = pos >= begin
            start_i = jnp.where(inside, begin, start_i)
            share_i = jnp.where(inside, share[d], share_i)
            begin = begin + lens[d]
        w_at = PRE + halves[h] * ROWS
        lim[h, 0:1, :] = jnp.where(share_i == 1, lens[0], 0)
        lim[h, 1:2, :] = start_i - base - w_at
        lim[h, 2:3, :] = pos - base - w_at

    one = jnp.where(alone, 1, 0)
    pl.semaphore_wait(barrier, 14 + jnp.where(source, 4 - one, 0) + jnp.where(spreads, 1 - one, 0))

    sends, arrivals = {}, {}

    def remote(name, src, dst, to, sent=None):
        at = arrivals.setdefault(name, len(arrivals))
        out = sends.setdefault(name if sent is None else sent, len(sends))
        return pltpu.make_async_remote_copy(
            src_ref=src, dst_ref=dst, send_sem=send.at[out], recv_sem=recv.at[at],
            device_id=to, device_id_type=MESH,
        )

    def arrived(name, size):
        pltpu.make_async_copy(size, size, recv.at[arrivals[name]]).wait()

    def left(name, size):
        pltpu.make_async_copy(size, size, send.at[sends[name]]).wait()

    def size_of(count):
        return kv.at[0, 0, 0:count, :]


    def columns(ref, to, g):
        return ref.at[:, pl.ds(pl.multiple_of((to * GROUPS + g) * HD, HD), HD)]

    def kv_head(g, i, n):
        ref = (k_ref, v_ref)[n]
        to = (peers + [y])[i]
        src = ref.at[:, pl.ds(pl.multiple_of((to * GROUPS + g) * HD, HD), HD)]
        dst = kv.at[g, n, pl.ds(own + mine, BLK), :]
        if i == 3:
            return pltpu.make_async_copy(src, dst, local.at[g * 2 + n])
        return remote(("kv", g), src, dst, device(slab, core, to))

    def q_head(g, i, n):
        ref, into = ((q_ref, q_in), (do_ref, do_in))[n]
        to = (peers + [y])[i]
        src = ref.at[:, pl.ds(pl.multiple_of((to * GROUPS + g) * WIDE, WIDE), WIDE)]
        dst = into.at[g, pl.ds(mine, BLK), :]
        if i == 3:
            return pltpu.make_async_copy(src, dst, local.at[4 + g * 2 + n])
        return remote(("q", g, n), src, dst, device(slab, core, to))

    def rows(g, at, count):
        return kv.at[g, :, pl.ds(at, count), :]

    def move(name, g, src, dst, count, to):
        return remote((name, g), rows(g, src, count), rows(g, dst, count), to)

    def unit_at(u):
        return pl.multiple_of((core + 2 * u) * UNIT, UNIT)

    def spread_in(g, step, n):
        src = columns((k_ref, v_ref)[n], (y + step) % 4, g)
        dst = kv.at[g, n, pl.ds(pl.multiple_of(unit_at(x) + mine, BLK), BLK), :]
        return remote(
            ("in",), src, dst, device(y * 4 + x, core, (y + step) % 4), sent=("ins", step > 0)
        )

    def spread_own(g, n):
        src = columns((k_ref, v_ref)[n], y, g)
        return pltpu.make_async_copy(
            src, kv.at[g, n, pl.ds(pl.multiple_of(unit_at(x) + mine, BLK), BLK), :], local.at[18 + g * 2 + n]
        )

    def quarter(u):
        return kv.at[:, :, pl.ds(pl.multiple_of(unit_at(u) + z * QUARTER, QUARTER), QUARTER), :]

    def along_x(u, step):
        return remote(
            ("x", u, step), quarter(u), quarter(u), device(z * 4 + (u + step) % 4, core, y), sent=("xs",)
        )

    def along_z(g, u, step):
        at = pl.multiple_of(unit_at(u) + z * QUARTER, QUARTER)
        return move("z", g, at, at, QUARTER, device((slab + 4 * step) % 16, core, y))

    def half_unit(g, u):
        return move(("half", u), g, unit_at(u), unit_at(u), UNIT, sibling)

    def window(g, ahead):
        return move(
            ("window", ahead), g, own, slot[2] if ahead == 1 else slot[0], UNIT,
            device((slab + ahead) % 16, core, y),
        )

    def core_own(g):
        return move(("core", 3), g, own, slot[3], UNIT, sibling)

    def near_up(g):
        return move(("core", 1), g, slot[2], slot[1], UNIT, sibling)

    def near_down(g):
        return move(("core", 3), g, slot[2], slot[3], UNIT, sibling)

    def far_down(g):
        return move(("core", 1), g, slot[0], slot[1], UNIT, sibling)

    def q_start(g, n):
        for i in (0, 3, 1, 2):
            q_head(g, i, n).start()

    def q_wait(g, n):
        arrived(("q", g, n), q_in.at[g, 0:3 * BLK, :])
        q_head(g, 3, n).wait()

    def kv_start(g):
        for i in range(4):
            for n in range(2):
                kv_head(g, i, n).start()

    def kv_units(g):
        arrived(("kv", g), size_of(6 * BLK))
        for n in range(2):
            kv_head(g, 3, n).wait()
        for ahead in (1, 2):
            @pl.when(slab + ahead < 16)
            def _():
                window(g, ahead).start()

        @pl.when(core == 0)
        def _():
            core_own(g).start()

    def pre_in():
        @pl.when(source)
        def _():
            for g in range(GROUPS):
                for n in range(2):
                    @pl.when(jnp.logical_not(alone))
                    def _():
                        spread_in(g, 0, n).start()

                    @pl.when(alone)
                    def _():
                        spread_own(g, n).start()

                    for step in range(1, 4):
                        spread_in(g, step, n).start()

    def pre_x():
        for u in range(2):
            @pl.when(x == u)
            def _():
                @pl.when(jnp.logical_not(alone))
                def _():
                    arrived(("in",), size_of(4 * BLK))

                @pl.when(alone)
                def _():
                    for g in range(GROUPS):
                        for n in range(2):
                            spread_own(g, n).wait()

                for step in (2, 1, 3):
                    along_x(u, step).start()

    def pre_z():
        for u in range(2):
            for step in range(1, 4):
                @pl.when(x == (u + step) % 4)
                def _():
                    along_x(u, step).wait_recv()
        for g in range(GROUPS):
            for step in (2, 1, 3):
                for u in range(2):
                    along_z(g, u, step).start()

    def pre_core(g):
        arrived(("z", g), size_of(12 * QUARTER))
        for u in range(2):
            half_unit(g, u).start()

    def pre_done(g):
        for u in range(2):
            half_unit(g, u).wait_recv()

    def win_core(g):
        @pl.when(slab >= 1)
        def _():
            window(g, 1).wait_recv()

            @pl.when(core == 0)
            def _():
                near_up(g).start()

            @pl.when(core == 1)
            def _():
                near_down(g).start()

        @pl.when(slab >= 2)
        def _():
            window(g, 2).wait_recv()

            @pl.when(core == 1)
            def _():
                far_down(g).start()

    def win_done(g):
        @pl.when(core == 1)
        def _():
            core_own(g).wait_recv()

            @pl.when(slab >= 1)
            def _():
                near_up(g).wait_recv()

        @pl.when(core == 0)
        def _():
            @pl.when(slab >= 1)
            def _():
                near_down(g).wait_recv()

            @pl.when(slab >= 2)
            def _():
                far_down(g).wait_recv()


    def q_back(g, i, n):
        buf, ref = ((out_buf, o_ref), (dq_buf, odq_ref))[n]
        to = (peers + [y])[i]
        src = buf.at[g, pl.ds(pl.multiple_of(to * BLK, BLK), BLK), :]
        dst = ref.at[:, pl.ds(pl.multiple_of((y * GROUPS + g) * WIDE, WIDE), WIDE)]
        if i == 3:
            return pltpu.make_async_copy(src, dst, local.at[10 + g * 2 + n])
        return remote(("back", g, n), src, dst, device(slab, core, to))

    def core_sum(g, i):
        at = unit_at(i) + (1 - 2 * core) * UNIT if i < 2 else slot[1 + 2 * (i - 2)]
        if i < 2:
            at = pl.multiple_of(at, UNIT)
        return remote(("csum", g, i), g_buf.at[g, :, pl.ds(at, UNIT), :], core_buf.at[g, i], sibling)

    def z_sum(g, step):
        at = pl.multiple_of(((z + step) % 4) * QUARTER, QUARTER)
        return remote(
            ("zsum", g), z_send.at[g, :, :, pl.ds(at, QUARTER), :], z_buf.at[g, step - 1],
            device((slab + 4 * step) % 16, core, y),
        )

    def x_sum(g, u, step):
        return remote(
            ("xsum", g, step), x_send.at[g, u], x_buf.at[g, step - 1], device(z * 4 + u, core, y),
            sent=("xsums", g, u),
        )

    def home(g, step):
        at = pl.multiple_of(z * QUARTER, QUARTER)
        return remote(
            ("home", g, step), last_send.at[g], last_buf.at[g, :, pl.ds(at, QUARTER), :], device(x, core, y),
            sent=("homes", g),
        )

    def w_sum(g, back):
        return remote(
            ("wsum", g, back), w_send.at[g, back - 1], w_buf.at[g, back - 1],
            device((slab + 16 - back) % 16, core, y),
        )

    def k_back(g, i, n):
        ref = (dk_ref, dv_ref)[n]
        to = (peers + [y])[i]
        src = k_buf.at[g, n, pl.ds(pl.multiple_of(to * BLK, BLK), BLK), :]
        dst = ref.at[:, pl.ds(pl.multiple_of((y * GROUPS + g) * HD, HD), HD)]
        if i == 3:
            return pltpu.make_async_copy(src, dst, local.at[14 + g * 2 + n])
        return remote(("kback", g), src, dst, device(slab, core, to))

    def pre_sum_core(g):
        for i in range(2):
            core_sum(g, i).start()

    def pre_sum_z(g):
        for i in range(2):
            core_sum(g, i).wait_recv()
            z_send[g, i] = (
                g_buf[g, :, pl.ds(unit_at(i), UNIT), :].astype(F32) + core_buf[g, i].astype(F32)
            ).astype(BF)
        for step in range(1, 4):
            z_sum(g, step).start()

    def pre_sum_x(g):
        arrived(("zsum", g), z_buf.at[g])
        total = z_send[g, :, :, pl.ds(pl.multiple_of(z * QUARTER, QUARTER), QUARTER), :].astype(F32)
        for i in range(3):
            total += z_buf[g, i].astype(F32)
        x_send[g] = total.astype(BF)
        for u in range(2):
            for step in range(1, 4):
                @pl.when(x == (u + step) % 4)
                def _():
                    x_sum(g, u, step).start()

    def pre_sum_home(g):
        for u in range(2):
            @pl.when(x == u)
            def _():
                total = x_send[g, u].astype(F32)
                for step in range(1, 4):
                    x_sum(g, u, step).wait_recv()
                    total += x_buf[g, step - 1].astype(F32)
                last_send[g] = total.astype(BF)
                for step in range(1, 4):
                    @pl.when(z == step)
                    def _():
                        home(g, step).start()

    def win_sum_core(g):
        for i in (2, 3):
            core_sum(g, i).start()

    def win_sum_x(g):
        core_sum(g, 2).wait_recv()
        core_sum(g, 3).wait_recv()
        a = core_buf[g, 2].astype(F32)
        b = core_buf[g, 3].astype(F32)
        lower = core == 0
        far = g_buf[g, :, slot[0]:slot[0] + UNIT, :].astype(F32)
        near = g_buf[g, :, slot[2]:slot[2] + UNIT, :].astype(F32)
        here = g_buf[g, :, slot[4]:slot[4] + UNIT, :].astype(F32)
        w_send[g, 1] = (far + jnp.where(lower, 0.0, a)).astype(BF)
        w_send[g, 0] = (near + jnp.where(lower, a, b)).astype(BF)
        for back in (2, 1):
            @pl.when(slab >= back)
            def _():
                w_sum(g, back).start()
        sum_buf[g] = here + jnp.where(lower, b, 0.0)

    def sum_back(g):
        @pl.when(slab < 2)
        def _():
            for step in range(1, 4):
                home_at = step * QUARTER
                remote(
                    ("home", g, step), last_send.at[g], last_buf.at[g, :, pl.ds(home_at, QUARTER), :], sibling,
                    sent=("homes", g),
                ).wait_recv()
            last_buf[g, :, 0:QUARTER, :] = last_send[g]
            sum_buf[g] += last_buf[g].astype(F32)

        for back in (1, 2):
            @pl.when(slab + back < 16)
            def _():
                w_sum(g, back).wait_recv()
                sum_buf[g] += w_buf[g, back - 1].astype(F32)

        k_buf[g] = sum_buf[g].astype(BF)
        for i in (2, 1, 0, 3):
            for n in range(2):
                k_back(g, i, n).start()


    def blocks_of(part, h):
        if part == 0:
            return [(at, at, KC) for at in range(0, PRE, KC)]
        w_at = PRE + halves[h] * ROWS
        blocks = [(pl.multiple_of(w_at + at, ROWS), at, KC) for at in range(0, BACK * UNIT, KC)]
        return blocks + [(pl.multiple_of(w_at + BACK * UNIT, ROWS), BACK * UNIT, ROWS)]

    def place(h):
        return pl.ds(pl.multiple_of(halves[h] * ROWS, ROWS), ROWS)

    def scores(g, h, part, state):
        state["top"] = jnp.full((8, LANES), -1e30, F32)

        def step(src, at, count):
            s = lax.dot_general(
                kv[g, 0, pl.ds(src, count), :], q_scr[g, h], NT, preferred_element_type=F32
            )
            j = lax.broadcasted_iota(jnp.int32, (count, LANES), 0)
            if part == 0:
                ok = j < lim[h, 0:1, :] - at
            else:
                ok = j >= lim[h, 1:2, :] - at
                if count == ROWS:
                    ok &= j <= lim[h, 2:3, :] - at
            s = jnp.where(ok, s, -1e30)
            s_scr[h, at:at + count, :] = s
            state["top"] = jnp.maximum(state["top"], jnp.max(s.reshape(count // 8, 8, LANES), axis=0))

        return [lambda b=b: step(*b) for b in blocks_of(part, h)]

    def weighted(g, h, part, state):
        p_scr = (p_pre, p_win)[part]

        def step(src, at, count):
            if at == 0:
                state["mc"] = jnp.max(state["top"], axis=0, keepdims=True) * (SCALE * LOG2E)
                state["sum"] = jnp.zeros((8, LANES), F32)
            p = jnp.exp2(s_scr[h, at:at + count, :] * (SCALE * LOG2E) - state["mc"])
            state["sum"] += jnp.sum(p.reshape(count // 8, 8, LANES), axis=0)
            pb = p.astype(BF)
            p_scr[g, h, at:at + count, :] = pb
            o = jnp.dot(kt[g, 1, :, pl.ds(src, count)], pb, preferred_element_type=F32)
            spot = acc.at[part, g, h]
            if at == 0:
                spot[...] = o
            else:
                spot[...] += o

        return [lambda b=b: step(*b) for b in blocks_of(part, h)]

    def turn(g, low, count):
        for n in range(2):
            kt[g, n, :, low:low + count] = kv[g, n, low:low + count, :].astype(F32).T.astype(BF)

    def both(g, part):
        state = [{}, {}]
        for step in scores(g, 0, part, state[0]):
            step()
        late = scores(g, 1, part, state[1])
        for step in weighted(g, 0, part, state[0]):
            late.pop(0)()
            step()
        for step in weighted(g, 1, part, state[1]):
            step()
        return state

    def window_forward(g):
        for h in range(2):
            for i in range(PER):
                q_scr[g, h, i * ROWS:(i + 1) * ROWS, :] = q_in[g, place(h), i * HD:(i + 1) * HD]
        turn(g, PRE, KEYS - PRE)
        state = both(g, 1)
        for h in range(2):
            stat[g, h, 0:1, :] = state[h]["mc"]
            stat[g, h, 1:2, :] = jnp.sum(state[h]["sum"], axis=0, keepdims=True)

    def prefix_forward(g):
        turn(g, 0, PRE)
        state = both(g, 0)
        for h in range(2):
            mw = stat[g, h, 0:1, :]
            lw = stat[g, h, 1:2, :]
            mp = state[h]["mc"]
            lp = jnp.sum(state[h]["sum"], axis=0, keepdims=True)
            m = jnp.maximum(mw, mp)
            aw = jnp.exp2(mw - m)
            ap = jnp.exp2(mp - m)
            inv = 1.0 / (aw * lw + ap * lp)
            fp = ap * inv
            fw = aw * inv
            stat[g, h, 0:1, :] = fp
            stat[g, h, 1:2, :] = fw
            o = acc[0, g, h] * fp + acc[1, g, h] * fw
            out_t[g, h] = o.astype(BF)
            out = o.T.astype(BF)
            for i in range(PER):
                out_buf[g, place(h), i * HD:(i + 1) * HD] = out[i * ROWS:(i + 1) * ROWS, :]

    def gradients(g, h, part):
        p_scr = (p_pre, p_win)[part]
        if part == 0:
            for i in range(PER):
                do_t[g, h, :, i * ROWS:(i + 1) * ROWS] = (
                    do_in[g, place(h), i * HD:(i + 1) * HD].astype(F32).T.astype(BF)
                )
        factor = stat[g, h, part:part + 1, :]
        scaled = (do_t[g, h].astype(F32) * factor).astype(BF)
        dot_scr[h] = scaled
        delta = jnp.sum(scaled.astype(F32) * out_t[g, h].astype(F32), axis=0, keepdims=True)
        first_half = h == (0 if part == 0 else 1)
        for src, at, count in blocks_of(part, h):
            dp = jnp.dot(kv[g, 1, pl.ds(src, count), :], dot_scr[h], preferred_element_type=F32)
            pb = p_scr[g, h, at:at + count, :]
            ds = (pb.astype(F32) * (dp - delta)).astype(BF)
            tv = lax.dot_general(pb, dot_scr[h], NT, preferred_element_type=F32)
            tk = jnp.dot(ds, q_scr[g, h], preferred_element_type=F32)
            if first_half:
                gv[pl.ds(src, count), :] = tv
                gk[pl.ds(src, count), :] = tk
            else:
                g_buf[g, 1, pl.ds(src, count), :] = (gv[pl.ds(src, count), :] + tv).astype(BF)
                g_buf[g, 0, pl.ds(src, count), :] = ((gk[pl.ds(src, count), :] + tk) * SCALE).astype(BF)
            p_scr[g, h, at:at + count, :] = ds

    def window_backward(g, h):
        apart = [pl.ds(pl.multiple_of(PRE + halves[1 - i] * SPAN, ROWS), ROWS) for i in range(2)]
        if h == 1:
            zero = jnp.zeros((ROWS, HD), F32)
            gk[apart[1], :] = zero
            gv[apart[1], :] = zero
        gradients(g, h, 1)
        if h == 0:
            g_buf[g, 1, apart[0], :] = gv[apart[0], :].astype(BF)
            g_buf[g, 0, apart[0], :] = (gk[apart[0], :] * SCALE).astype(BF)

    def query_gradients(g, h):
        w_at = pl.multiple_of(PRE + halves[h] * ROWS, ROWS)
        o = jnp.dot(kt[g, 0, :, 0:PRE], p_pre[g, h], preferred_element_type=F32)
        o += jnp.dot(kt[g, 0, :, pl.ds(w_at, SPAN)], p_win[g, h], preferred_element_type=F32)
        dq = (o * SCALE).T.astype(BF)
        for i in range(PER):
            dq_buf[g, place(h), i * HD:(i + 1) * HD] = dq[i * ROWS:(i + 1) * ROWS, :]


    def each_group(before, work, after):
        def body(g, carry):
            for k in range(GROUPS):
                @pl.when(g == k)
                def _():
                    before(k)
            work(g)
            for k in range(GROUPS):
                @pl.when(g == k)
                def _():
                    after(k)
            return carry

        lax.fori_loop(0, GROUPS, body, 0)

    pre_in()
    kv_start(0)
    kv_start(1)
    q_start(0, 0)
    pre_x()
    kv_units(0)
    pre_z()
    kv_units(1)
    q_start(1, 0)
    q_start(0, 1)
    q_start(1, 1)
    win_core(0)

    def before_wf(g):
        if g == 1:
            win_core(1)
        q_wait(g, 0)
        win_done(g)

    def after_wf(g):
        if g == 0:
            pre_core(0)

    each_group(before_wf, window_forward, after_wf)

    def before_pf(g):
        if g == 0:
            pre_core(1)
        pre_done(g)

    def after_pf(g):
        for i in (1, 2, 0, 3):
            q_back(g, i, 0).start()

    each_group(before_pf, prefix_forward, after_pf)

    def after_pb(g, h):
        if h == 1:
            pre_sum_core(g)
        if (g, h) == (1, 0):
            pre_sum_z(0)

    def after_wb(g, h):
        if (g, h) == (0, 1):
            pre_sum_z(1)
        if (g, h) == (0, 0):
            win_sum_core(0)
        if (g, h) == (1, 1):
            pre_sum_x(1)
        if (g, h) == (1, 0):
            win_sum_core(1)
            pre_sum_home(0)

    def after_dq(g, h):
        if (g, h) == (1, 1):
            win_sum_x(1)
        for i in of_half[h]:
            q_back(g, i, 1).start()
        if (g, h) == (0, 1):
            pre_sum_x(0)
        if (g, h) == (0, 0):
            win_sum_x(0)
        if (g, h) == (1, 1):
            pre_sum_home(1)
        if (g, h) == (1, 0):
            sum_back(0)
            sum_back(1)

    def at_group(g, h, after):
        for k in range(GROUPS):
            @pl.when(g == k)
            def _():
                after(k, h)

    def pb_body(g, carry):
        for k in range(GROUPS):
            @pl.when(g == k)
            def _():
                q_wait(k, 1)
        for h in (0, 1):
            gradients(g, h, 0)
            at_group(g, h, after_pb)
        return carry

    def wb_body(g, carry):
        for work, after in ((window_backward, after_wb), (query_gradients, after_dq)):
            for h in (1, 0):
                work(g, h)
                at_group(g, h, after)
        return carry

    lax.fori_loop(0, GROUPS, pb_body, 0)
    lax.fori_loop(0, GROUPS, wb_body, 0)


    for g in range(GROUPS):
        for n in range(2):
            arrived(("back", g, n), out_buf.at[g, 0:3 * BLK, :])
            q_back(g, 3, n).wait()
            k_back(g, 3, n).wait()
            left(("q", g, n), q_in.at[g, 0:3 * BLK, :])
            left(("back", g, n), out_buf.at[g, 0:3 * BLK, :])
        arrived(("kback", g), size_of(6 * BLK))
        left(("kback", g), size_of(6 * BLK))
        left(("kv", g), size_of(6 * BLK))
        left(("z", g), size_of(12 * QUARTER))
        left(("zsum", g), z_buf.at[g])
        for step in range(1, 4):
            for u in range(2):
                @pl.when(x == (u + step) % 4)
                def _():
                    x_sum(g, u, step).wait_send()

            @pl.when((x < 2) & (z == step))
            def _():
                home(g, step).wait_send()

        for u in range(2):
            half_unit(g, u).wait_send()
        for i in range(4):
            core_sum(g, i).wait_send()

        for ahead in (1, 2):
            @pl.when(slab + ahead < 16)
            def _():
                window(g, ahead).wait_send()

            @pl.when(slab >= ahead)
            def _():
                w_sum(g, ahead).wait_send()

        @pl.when(core == 0)
        def _():
            core_own(g).wait_send()

            @pl.when(slab >= 1)
            def _():
                near_up(g).wait_send()

        @pl.when(core == 1)
        def _():
            @pl.when(slab >= 1)
            def _():
                near_down(g).wait_send()

            @pl.when(slab >= 2)
            def _():
                far_down(g).wait_send()

    @pl.when(source)
    def _():
        left(("ins", True), size_of(12 * BLK))

        @pl.when(jnp.logical_not(alone))
        def _():
            left(("ins", False), size_of(4 * BLK))

    @pl.when(spreads)
    def _():
        left(("xs",), size_of(12 * QUARTER))

    assert (len(sends), len(arrivals)) == (SENDS, ARRIVALS), (len(sends), len(arrivals))


def store_kernel(*refs):
    src, dst, held = refs[:4], refs[4:8], refs[8:12]
    into, out = refs[12:]
    parts = [(a, b * BLK // n, BLK // n, b) for a, n in enumerate((4, 4, 1, 1)) for b in range(n)]

    def load(a, at, count, b):
        return pltpu.make_async_copy(src[a].at[pl.ds(at, count)], held[a].at[pl.ds(at, count)], into.at[a, b])

    def save(a, at, count, b):
        return pltpu.make_async_copy(held[a].at[pl.ds(at, count)], dst[a].at[pl.ds(at, count)], out.at[a, b])

    for part in parts:
        load(*part).start()
    for part in parts:
        load(*part).wait()
        save(*part).start()
    for part in parts:
        save(*part).wait()


def on_device(queries, keys, values, grad_out, doc_lengths, share_prefix):
    anywhere = pl.BlockSpec(memory_space=pl.ANY)
    smem = pl.BlockSpec(memory_space=pltpu.SMEM)
    unit = (2, UNIT, HD)
    G = GROUPS
    results = pl.pallas_call(
        kernel,
        in_specs=[smem, smem] + [anywhere] * 4,
        out_specs=[anywhere] * 4,
        out_shape=[
            jax.ShapeDtypeStruct((BLK, QH * HD), BF),
            jax.ShapeDtypeStruct((BLK, QH * HD), BF),
            jax.ShapeDtypeStruct((BLK, KVH * HD), BF),
            jax.ShapeDtypeStruct((BLK, KVH * HD), BF),
        ],
        scratch_shapes=[
            pltpu.VMEM((G, UNIT, WIDE), BF),
            pltpu.VMEM((G, UNIT, WIDE), BF),
            pltpu.VMEM((G, 2, KEYS, HD), BF),
            pltpu.VMEM((G, 2, HD, KEYS), BF),
            pltpu.VMEM((2, SPAN, LANES), F32),
            pltpu.VMEM((G, 2, SPAN, LANES), BF),
            pltpu.VMEM((G, 2, PRE, LANES), BF),
            pltpu.VMEM((G, 2, LANES, HD), BF),
            pltpu.VMEM((2, HD, LANES), BF),
            pltpu.VMEM((2, G, 2, HD, LANES), F32),
            pltpu.VMEM((G, 2, HD, LANES), BF),
            pltpu.VMEM((G, 2, HD, LANES), BF),
            pltpu.VMEM((2, 8, LANES), jnp.int32),
            pltpu.VMEM((G, 2, 8, LANES), F32),
            pltpu.VMEM((KEYS, HD), F32),
            pltpu.VMEM((KEYS, HD), F32),
            pltpu.VMEM((G, UNIT, WIDE), BF),
            pltpu.VMEM((G, UNIT, WIDE), BF),
            pltpu.VMEM((G, 2, KEYS, HD), BF),
            pltpu.VMEM((G, 4) + unit, BF),
            pltpu.VMEM((G, 2) + unit, BF),
            pltpu.VMEM((G, 3, 2, 2, QUARTER, HD), BF),
            pltpu.VMEM((G, 2, 2, QUARTER, HD), BF),
            pltpu.VMEM((G, 3, 2, QUARTER, HD), BF),
            pltpu.VMEM((G, 2, QUARTER, HD), BF),
            pltpu.VMEM((G,) + unit, BF),
            pltpu.VMEM((G, 2) + unit, BF),
            pltpu.VMEM((G, 2) + unit, BF),
            pltpu.VMEM((G,) + unit, F32),
            pltpu.VMEM((G,) + unit, BF),
            pltpu.SemaphoreType.DMA((SENDS,)),
            pltpu.SemaphoreType.DMA((ARRIVALS,)),
            pltpu.SemaphoreType.DMA((22,)),
        ],
        compiler_params=pltpu.CompilerParams(
            collective_id=0, has_side_effects=True, vmem_limit_bytes=60 * 1024 * 1024
        ),
        name="packed_attention",
    )(doc_lengths, share_prefix, queries, grad_out, keys, values)
    return tuple(pl.pallas_call(
        store_kernel,
        in_specs=[anywhere] * 4,
        out_specs=[anywhere] * 4,
        out_shape=[jax.ShapeDtypeStruct(a.shape, a.dtype) for a in results],
        scratch_shapes=[pltpu.VMEM(a.shape, a.dtype) for a in results] + [pltpu.SemaphoreType.DMA((4, 4))] * 2,
        name="store_results",
    )(*results))


def solution(mesh):
    rows = P(("ctx", "heads"), None)
    return jax.shard_map(
        on_device, mesh=mesh, in_specs=(rows, rows, rows, rows, P(), P()),
        out_specs=(rows, rows, rows, rows), check_vma=False,
    )
```
